512 devices in a mesh: replica: 64 (over z, x, core), tensor: 8 (over y).
Axes of the slice: x: 4, y: 8, z: 8, core: 2. Of those that a mesh axis runs over, the one named last changes fastest.
Arguments:
- tokens: bfloat16 [1024, 4, 8192], P('replica', None, 'tensor'), may hold values from -6 to 6
- value_matrix: bfloat16 [8192, 1024], P(None, 'tensor'), may hold values from -0.0625 to 0.0625
- queries: bfloat16 [1024, 4, 8192], P('replica', None, 'tensor'), may hold values from -400 to 400, as said below
- draft_keys: bfloat16 [1024, 4, 1024], P('replica', None, 'tensor'), may hold values from -6 to 6
- key_cache_before: bfloat16 [1024, 64, 1024], P('replica', None, 'tensor'), may hold values from -6 to 6
- value_cache_before: bfloat16 [1024, 64, 1024], P('replica', None, 'tensor'), may hold values from -6 to 6
- cache_length: int32 [1024], P('replica'), may hold values from 1 to 60, as said below
- migrations: int32 [64, 3, 3], P('replica'), may hold values from 0 to 63, as said below
- block_adapter_index: int32 [64, 4], P('replica'), may hold values from 0 to 63, as said below
- adapter_replica: int32 [64], replicated, may hold values from 0 to 63, as said below
- adapter_shrink: bfloat16 [64, 8192, 64], P('replica', 'tensor'), may hold values from -0.0625 to 0.0625
- adapter_expand: bfloat16 [64, 64, 1024], P('replica', None, 'tensor'), may hold values from -0.75 to 0.75
Outputs:
- attended: bfloat16 [1024, 4, 8192], P('replica', None, 'tensor')
- keys_out: bfloat16 [1024, 64, 1024], P('replica', None, 'tensor')
- values_out: bfloat16 [1024, 64, 1024], P('replica', None, 'tensor')
The draws below stay inside these ranges and needn't reach their ends.
Inputs may be any that keep to these rules, and one draw needn't show every extreme that they name: `queries`: each draft token's query features; their scale may differ from head to head. `cache_length`: every request has room for its 4 draft tokens. `migrations`: row q lists the 3 requests leaving replica q as (slot on q, destination replica, slot on the destination), at distinct slots of q. Every replica uses the same 3 distinct nonzero offsets from source to destination, counted round the replicas; one of them is 1 and one is half the number of replicas. So every replica sends and receives exactly 3 requests, at most one to or from each peer, and each slot it gives up receives exactly one arriving request. `block_adapter_index`: adapter ids of the blocks; some adapters are used by many blocks. `adapter_replica`: each replica holds exactly one adapter.
All inputs are finite; a program needn't handle non-finite values.
Results may differ from the reference program's by a relative error of at most 0.0054.
Values may be sent and summed in bfloat16 or wider, within the bound.
A program may use at most 64 MiB of HBM per device.

```python
import math
import jax
import jax.numpy as jnp
from jax import lax

MODEL_WIDTH = 8192
HEADS = 64
KV_HEADS = 8
HD = 128
ADAPTER_RANK = 64
STEPS = 4
BLOCK_SLOTS = 4
MIG = 3
SLOTS = 16
CACHE = 64
REQUESTS = 1024
BLOCKS = 4
ADAPTER_COUNT = 64
KEY_VALUE_WIDTH = 1024
N_REPLICA = 64


def owner_layout(key):
    return jax.random.permutation(key, ADAPTER_COUNT).astype(jnp.int32)


def draw_adapter_replica(key, part):
    owners = owner_layout(key)
    return owners


def draw_block_adapter_index(key, part):
    owners = owner_layout(key)
    key = jax.random.fold_in(key, 23)
    first, second, third, fourth = jax.random.split(key, 4)
    popular = jax.random.permutation(first, ADAPTER_COUNT).astype(jnp.int32)
    reach = jax.random.randint(second, (N_REPLICA, BLOCKS), 0, ADAPTER_COUNT)
    ranks = jax.random.randint(third, (N_REPLICA, BLOCKS), 0, reach + 1)
    chosen = popular[ranks]
    owned_by = jnp.zeros((ADAPTER_COUNT,), jnp.int32).at[owners].set(jnp.arange(ADAPTER_COUNT, dtype=jnp.int32))
    start = jax.random.randint(fourth, (), 0, N_REPLICA)
    half = N_REPLICA // 2
    chosen = chosen.at[start % N_REPLICA, 0].set(owned_by[(start - 1) % N_REPLICA])
    chosen = chosen.at[(start + 1) % N_REPLICA, BLOCKS - 1].set(owned_by[(start + 1 + half) % N_REPLICA])
    chosen = chosen.at[(start + 2) % N_REPLICA, 0].set(owned_by[(start + 3) % N_REPLICA])
    return chosen.astype(jnp.int32)


def draw_queries(key, part):
    key = jax.random.fold_in(key, 7)
    first = jax.random.fold_in(key, 0)
    values = jax.random.normal(first, (REQUESTS, STEPS, HEADS, HD), jnp.float32)
    values = jnp.clip(values, -6.0, 6.0)
    return values.reshape(REQUESTS, STEPS, HEADS * HD).astype(jnp.bfloat16)


def draw_cache_length(key, part):
    key = jax.random.fold_in(key, 13)
    first, second, third = jax.random.split(key, 3)
    ceiling = CACHE - STEPS
    limits = jax.random.randint(first, (N_REPLICA, 1), max(ceiling // 4, 1), ceiling + 1)
    lengths = jax.random.randint(second, (N_REPLICA, SLOTS), 1, limits + 1).reshape(-1)
    chosen = jax.random.randint(third, (), 0, N_REPLICA * SLOTS)
    lengths = jnp.where(jnp.arange(N_REPLICA * SLOTS) == chosen, ceiling, lengths)
    return lengths.astype(jnp.int32)


def draw_migrations(key, part):
    key = jax.random.fold_in(key, 17)
    first, second, third = jax.random.split(key, 3)
    half = N_REPLICA // 2
    other = jax.random.randint(first, (), 0, N_REPLICA - 3) + 2
    other = jnp.where(other >= half, other + 1, other)
    offsets = jnp.stack([jnp.array(half, jnp.int32), jnp.array(1, jnp.int32), other.astype(jnp.int32)])
    offsets = jax.random.permutation(second, offsets)[:MIG].astype(jnp.int32)
    slot_keys = jax.random.split(third, N_REPLICA)
    orders = jax.vmap(lambda single: jax.random.permutation(single, SLOTS))(slot_keys)[:, :MIG].astype(jnp.int32)
    source = jnp.arange(N_REPLICA, dtype=jnp.int32)[:, None]
    target = (source + offsets[None, :]) % N_REPLICA
    target_slot = orders[target, jnp.arange(MIG)[None, :]]
    return jnp.stack([orders, target, target_slot], axis=-1).astype(jnp.int32)


def shard_levels(stream_key, extent, shards, least, high):
    factor_of, own = 1.0, jax.random.fold_in(stream_key, 6)
    for axis_at, blocks in shards:
        draws = jnp.exp(jax.random.uniform(jax.random.fold_in(own, axis_at), (blocks,), jnp.float32, least / len(shards), high / len(shards)))
        factor_of = factor_of * jnp.repeat(draws, extent[axis_at] // blocks).reshape([-1 if axis == axis_at else 1 for axis in range(len(extent))])
    return factor_of


def normal_values(rng, shape, scale, bound, shards=(), kind=jnp.bfloat16):
    result = scale * jax.random.normal(rng, shape, jnp.float32)
    if shards:
        result = result * shard_levels(rng, shape, shards, -0.22, 0.18)
    return jnp.clip(result, -bound, bound).astype(kind)


def setup_inputs(seed: int = 0) -> dict:
    key_of = jax.random.split(jax.random.key(seed), 13)
    return {
        "tokens": normal_values(key_of[0], (REQUESTS, STEPS, MODEL_WIDTH), 1.0, 6.0, ((0, 64), (2, 8))),
        "value_matrix": normal_values(key_of[1], (MODEL_WIDTH, KEY_VALUE_WIDTH), MODEL_WIDTH ** -0.5, 0.0625, ((1, 8),)),
        "queries": draw_queries(jax.random.fold_in(key_of[12], 71), 0),
        "draft_keys": normal_values(key_of[3], (REQUESTS, STEPS, KEY_VALUE_WIDTH), 1.0, 6.0, ((0, 64), (2, 8))),
        "key_cache_before": normal_values(key_of[4], (REQUESTS, CACHE, KEY_VALUE_WIDTH), 1.0, 6.0, ((0, 64), (2, 8))),
        "value_cache_before": normal_values(key_of[5], (REQUESTS, CACHE, KEY_VALUE_WIDTH), 1.0, 6.0, ((0, 64), (2, 8))),
        "cache_length": draw_cache_length(jax.random.fold_in(key_of[12], 71), 0),
        "migrations": draw_migrations(jax.random.fold_in(key_of[12], 71), 0),
        "block_adapter_index": draw_block_adapter_index(jax.random.fold_in(key_of[12], 71), 0),
        "adapter_replica": draw_adapter_replica(jax.random.fold_in(key_of[12], 71), 0),
        "adapter_shrink": normal_values(key_of[10], (ADAPTER_COUNT, MODEL_WIDTH, ADAPTER_RANK), MODEL_WIDTH ** -0.5, 0.0625, ((0, 64), (1, 8))),
        "adapter_expand": normal_values(key_of[11], (ADAPTER_COUNT, ADAPTER_RANK, KEY_VALUE_WIDTH), ADAPTER_RANK ** -0.5, 0.75, ((0, 64), (2, 8))),
    }


def reference(tokens, value_matrix, queries, draft_keys, key_cache_before, value_cache_before, cache_length, migrations, block_adapter_index, adapter_replica, adapter_shrink, adapter_expand):
    requests = tokens.shape[0]
    slots = requests // N_REPLICA
    source = (jnp.arange(N_REPLICA, dtype=jnp.int32)[:, None] * slots + migrations[:, :, 0]).reshape(-1).astype(jnp.int32)
    target = (migrations[:, :, 1] * slots + migrations[:, :, 2]).reshape(-1).astype(jnp.int32)
    anchor = jnp.arange(requests, dtype=jnp.int32).at[target].set(source)
    moved_keys = key_cache_before[anchor]
    moved_values = value_cache_before[anchor]
    filled = cache_length[anchor]
    token_rows = tokens.reshape(requests * STEPS, MODEL_WIDTH)
    base = jnp.dot(token_rows, value_matrix, preferred_element_type=jnp.float32)
    blocks = requests // BLOCK_SLOTS
    block_rows = BLOCK_SLOTS * STEPS
    stored_at = adapter_replica[block_adapter_index.reshape(-1)].astype(jnp.int32)
    grouped = token_rows.reshape(blocks, block_rows, MODEL_WIDTH)

    def adapt(item):
        rows_here, token_position = item
        shrink_output = lax.dynamic_index_in_dim(adapter_shrink, token_position, 0, keepdims=False)
        upper_limit = lax.dynamic_index_in_dim(adapter_expand, token_position, 0, keepdims=False)
        shrink = jnp.dot(rows_here, shrink_output, preferred_element_type=jnp.float32).astype(jnp.bfloat16)
        return jnp.dot(shrink, upper_limit, preferred_element_type=jnp.float32)
    delta = lax.map(adapt, (grouped, stored_at)).reshape(requests * STEPS, KEY_VALUE_WIDTH)
    fresh_values = (base + delta).astype(jnp.bfloat16).reshape(requests, STEPS, KEY_VALUE_WIDTH)
    places = jnp.arange(CACHE, dtype=jnp.int32)
    step_ids = jnp.arange(STEPS, dtype=jnp.int32)
    token_position = filled[:, None] + step_ids[None, :]
    writes = places[None, :, None] == token_position[:, None, :]
    written = jnp.any(writes, axis=2)[:, :, None]
    write_weight = writes.astype(jnp.float32)
    keys_out = jnp.where(written, jnp.einsum('sln,snc->slc', write_weight, draft_keys.astype(jnp.float32)).astype(jnp.bfloat16), moved_keys)
    values_out = jnp.where(written, jnp.einsum('sln,snc->slc', write_weight, fresh_values.astype(jnp.float32)).astype(jnp.bfloat16), moved_values)
    group = HEADS // KV_HEADS
    shaped_q = queries.astype(jnp.float32).reshape(requests, STEPS, KV_HEADS, group, HD)
    shaped_k = keys_out.astype(jnp.float32).reshape(requests, CACHE, KV_HEADS, HD)
    scores = jnp.einsum('snkgd,slkd->snkgl', shaped_q, shaped_k) * (1.0 / math.sqrt(HD))
    allowed = (places[None, None, :] <= token_position[:, :, None])[:, :, None, None, :]
    masked = jnp.where(allowed, scores, -1e+30)
    top = lax.optimization_barrier(jnp.max(masked, axis=-1, keepdims=True))
    raised = jnp.where(allowed, jnp.exp(masked - top), 0.0)
    weights = (raised / lax.optimization_barrier(jnp.sum(raised, axis=-1, keepdims=True))).astype(jnp.bfloat16)
    shaped_v = values_out.astype(jnp.float32).reshape(requests, CACHE, KV_HEADS, HD)
    attended = jnp.einsum('snkgl,slkd->snkgd', weights.astype(jnp.float32), shaped_v)
    attended = attended.reshape(requests, STEPS, HEADS * HD).astype(jnp.bfloat16)
    return (attended, keys_out, values_out)
```

```python
import functools
import math

import jax
import jax.numpy as jnp
from jax import lax
from jax.experimental import pallas as pl
from jax.experimental.pallas import tpu as pltpu
from jax.sharding import PartitionSpec as P

NZ, NX, NC, NY = 8, 4, 2, 8
PLANE = NX * NC
REPLICAS = NZ * PLANE
MESH = pl.DeviceIdType.MESH
F32, BF16 = jnp.float32, jnp.bfloat16

SLOTS, STEPS, BLOCKS, CACHE, HD, RANK = 16, 4, 4, 64, 128, 64
ROWS = SLOTS * STEPS
PART = 1024
HALF = ROWS // 2
MIG_ROWS = 2 * CACHE + 16
COPIES = 110

SHRINK_AT = {1: 0, 7: 1, 2: 2, 6: 3, 3: 4, 5: 5, 0: 6, 4: 7}
EXPAND_AT = {1: 0, 7: 1, 2: 2, 6: 3, 0: 4, 3: 5, 5: 6, 4: 7}
NEAR = 5


def pick(table, index):
    out = jnp.int32(table[0])
    for key, value in table.items():
        if key:
            out = jnp.where(index == key, jnp.int32(value), out)
    return out


def lanes(shape):
    return lax.broadcasted_iota(jnp.int32, shape, len(shape) - 1)


def comm_kernel(
    tok_ref, w_hbm, keys_ref, values_ref, length_ref, mig_ref, index_ref, owner_ref, shrink_ref, expand_ref,
    fresh_ref, arrived_ref,
    w_ref, w_sem, tok_f32, tok_y, tok_x, shrink_z, expand_x, mig_out, mig_in, mig_x, mig_z,
    acc, part_out, part_x, part_y, send_sem, recv_sem,
):
    r, t = lax.axis_index("replica"), lax.axis_index("tensor")
    z, w = r // PLANE, r % PLANE
    x, c = w // NC, w % NC

    def along_z(d):
        return ((r + d * PLANE) % REPLICAS, t)

    def along_y(d):
        return (r, (t + d) % NY)

    def in_plane(dx, dc):
        return (z * PLANE + ((x + dx) % NX) * NC + (c + dc) % NC, t)

    copies = []

    def send(src, dst, device):
        k = len(copies)
        copy = pltpu.make_async_remote_copy(
            src_ref=src, dst_ref=dst, send_sem=send_sem.at[k], recv_sem=recv_sem.at[k],
            device_id=device, device_id_type=MESH,
        )
        copies.append(copy)
        copy.start()
        return copy

    load_w = pltpu.make_async_copy(w_hbm, w_ref, w_sem)
    load_w.start()

    barrier = pltpu.get_barrier_semaphore()
    others = [along_y(d) for d in range(1, NY)]
    others += [in_plane(dx, dc) for dx in range(NX) for dc in range(NC) if dx or dc]
    others += [along_z(1), along_z(-1), along_z(NZ // 2)]
    others += [((r + 1) % REPLICAS, t), ((r + REPLICAS - 1) % REPLICAS, t)]
    for other in others:
        pl.semaphore_signal(barrier, inc=1, device_id=other, device_id_type=MESH)

    for s in range(SLOTS):
        tok_f32[s * STEPS : (s + 1) * STEPS, :] = tok_ref[s].astype(F32)
    own = tok_f32[...].astype(BF16)
    tok_y[0] = own
    tok_x[0, :, 0:PART] = own
    row = lax.broadcasted_iota(jnp.int32, (ROWS, HD), 0)
    stored = [owner_ref[index_ref[0, b]] for b in range(BLOCKS)]
    stored_rows = jnp.zeros((ROWS, HD), F32)
    for b in range(BLOCKS):
        stored_rows = jnp.where(row // (ROWS // BLOCKS) == b, stored[b].astype(F32), stored_rows)
    tok_x[0, :, PART:] = stored_rows.astype(BF16)
    shrink_z[SHRINK_AT[0]] = shrink_ref[...]
    expand_x[0, EXPAND_AT[0]] = expand_ref[0]

    offsets = [(mig_ref[0, e, 1] - r + REPLICAS) % REPLICAS for e in range(3)]
    half = REPLICAS // 2
    fits = [
        [o == 1 for o in offsets],
        [o == half for o in offsets],
        [(o != 1) & (o != half) for o in offsets],
    ]

    def chosen(which, column):
        first, second, third = (column(e) for e in range(3))
        return jnp.where(fits[which][0], first, jnp.where(fits[which][1], second, third))

    other_offset = chosen(2, lambda e: offsets[e])
    mig_row = lax.broadcasted_iota(jnp.int32, (16, HD), 0)
    for which in range(3):
        slot = chosen(which, lambda e: mig_ref[0, e, 0])
        landing = chosen(which, lambda e: mig_ref[0, e, 2]).astype(F32)
        filled = length_ref[slot].astype(F32)
        notes = jnp.where(mig_row == 0, landing, filled).astype(BF16)
        mig_out[which, 0:CACHE] = keys_ref[slot]
        mig_out[which, CACHE : 2 * CACHE] = values_ref[slot]
        mig_out[which, 2 * CACHE :] = notes

    pl.semaphore_wait(barrier, len(others))

    def ring(n, right, left, parts, split):
        gone = {}
        for k in range(1, n // 2 + 1):
            stay = []
            for h, (at, last) in enumerate(zip(parts, split)):
                for way, device in ((-1, right), (1, left)):
                    if k == n // 2 and last != way:
                        stay.append(gone[k - 1, h, way])
                        continue
                    if k > 1:
                        gone[k - 1, h, way].wait_recv()
                    src, dst = way * (k - 1) % n, way * k % n
                    gone[k, h, way] = send(at(src), at(dst), device)
            for copy in stay:
                copy.wait_recv()
            yield k - 1
        for (k, _, _), copy in gone.items():
            if k == n // 2:
                copy.wait_recv()
        yield n // 2

    def finish(steps):
        for _ in steps:
            pass

    first_rows, last_rows = pl.ds(0, HALF), pl.ds(HALF, HALF)

    def shrink_part(rows):
        return lambda d: shrink_z.at[SHRINK_AT[d], rows]

    z_steps = ring(
        NZ, along_z(1), along_z(-1),
        [shrink_part(first_rows), shrink_part(last_rows), lambda d: expand_x.at[0, EXPAND_AT[d]]],
        [-1, 1, -1],
    )
    y_steps = ring(
        NY, along_y(1), along_y(-1),
        [lambda d: tok_y.at[d, first_rows], lambda d: tok_y.at[d, last_rows]],
        [-1, 1],
    )
    x_steps = ring(
        NX, in_plane(1, 0), in_plane(-1, 0),
        [lambda d: tok_x.at[d * NC, first_rows], lambda d: tok_x.at[d * NC, last_rows]],
        [-1, 1],
    )

    base = None

    def add_base(d):
        nonlocal base
        rows = pl.multiple_of((t + d) % NY * PART, PART)
        term = jnp.dot(tok_y[d], w_ref[pl.ds(rows, PART), :], preferred_element_type=F32)
        base = term if base is None else base + term

    next(z_steps)
    next(y_steps)
    next(x_steps)
    to_sibling = [send(tok_x.at[0], tok_x.at[1], in_plane(0, 1))]
    mig_sent = {}
    for dx in range(NX):
        for dc in range(NC):
            if dx or dc:
                back = (-dx % NX) * NC + dc
                mig_sent[dx, dc] = send(mig_out.at[2], mig_x.at[back], in_plane(dx, dc))
    straight = [
        send(mig_out.at[0], mig_in.at[0], ((r + 1) % REPLICAS, t)),
        send(mig_out.at[1], mig_in.at[1], along_z(half // PLANE)),
    ]
    mig_x[0] = mig_out[2]
    load_w.wait()
    add_base(0)

    next(z_steps)
    next(y_steps)
    next(x_steps)
    add_base(1)
    add_base(NY - 1)
    finish(x_steps)
    to_sibling += [send(tok_x.at[d * NC], tok_x.at[d * NC + 1], in_plane(0, 1)) for d in range(1, NX)]

    for copy in mig_sent.values():
        copy.wait_recv()
    plane_offset, z_offset = other_offset % PLANE, other_offset // PLANE
    from_w = (w - plane_offset + PLANE) % PLANE
    carry = jnp.where(from_w + plane_offset >= PLANE, 1, 0)
    from_slot = (from_w // NC - x + NX) % NX * NC + (from_w % NC - c + NC) % NC
    mig_z[0] = mig_x[from_slot]
    mig_steps = ring(
        NZ, along_z(1), along_z(-1),
        [lambda d: mig_z.at[d, pl.ds(0, CACHE)], lambda d: mig_z.at[d, pl.ds(CACHE, MIG_ROWS - CACHE)]],
        [-1, 1],
    )

    next(z_steps)
    next(y_steps)
    next(mig_steps)
    expand_sent = [
        [
            send(expand_x.at[0, pl.ds(0, NEAR)], expand_x.at[(-dx % NX) * NC, pl.ds(0, NEAR)], in_plane(dx, 0))
            for dx in range(1, NX)
        ]
    ]
    expand_sibling = [send(expand_x.at[0, pl.ds(0, NEAR)], expand_x.at[1, pl.ds(0, NEAR)], in_plane(0, 1))]
    add_base(2)
    add_base(NY - 2)

    next(z_steps)
    next(y_steps)
    next(mig_steps)
    for copy in to_sibling:
        copy.wait_recv()

    lane = lanes((1, HD))
    stored_all = tok_x[:, :, PART:].reshape(PLANE * ROWS, HD).astype(F32)

    def add_products(pair):
        both = shrink_z[2 * pair : 2 * pair + 2].reshape(2 * RANK, PART)
        product = lax.dot_general(
            tok_x[:, :, 0:PART].reshape(PLANE * ROWS, PART), both, (((1,), (1,)), ((), ())),
            preferred_element_type=F32,
        )
        first, second = (
            ((r + d * PLANE) % REPLICAS).astype(F32) for d, at in SHRINK_AT.items() if at // 2 == pair
        )
        mine = stored_all == jnp.where(lane < RANK, first, second)
        return jnp.where(mine, product, 0.0)

    acc[...] = add_products(0)
    acc[...] += add_products(1)
    add_base(3)
    add_base(NY - 3)
    for dx in range(1, NX):
        expand_sent[0][dx - 1].wait_recv()
        at = -dx % NX * NC
        src = expand_x.at[at, pl.ds(0, NEAR)]
        expand_sibling.append(send(src, expand_x.at[at + 1, pl.ds(0, NEAR)], in_plane(0, 1)))
    next(mig_steps)
    acc[...] += add_products(2)
    next(z_steps)

    far = pl.ds(NEAR, NZ - NEAR)
    far_sent = [
        send(expand_x.at[0, far], expand_x.at[(-dx % NX) * NC, far], in_plane(dx, 0)) for dx in range(1, NX)
    ]
    expand_sibling.append(send(expand_x.at[0, far], expand_x.at[1, far], in_plane(0, 1)))

    total = (acc[...] + add_products(3)).reshape(PLANE, ROWS, HD)
    total = total + jnp.concatenate([total[:, :, RANK:], total[:, :, :RANK]], axis=-1)
    part_out[...] = jnp.where(lanes((PLANE, HALF, HD)) < RANK, total[:, :HALF], total[:, HALF:])
    part_sent = []
    for dx in range(NX):
        for dc in range(NC):
            if dx or dc:
                back = (-dx % NX) * NC + dc
                part_sent.append(send(part_out.at[dx * NC + dc], part_x.at[back], in_plane(dx, dc)))
    part_x[0] = part_out[0]
    next(y_steps)
    add_base(4)
    next(mig_steps)
    for copy in part_sent:
        copy.wait_recv()
    part_y[0] = jnp.sum(part_x[...], axis=0)
    over_y = [send(part_y.at[0], part_y.at[NY - d], along_y(d)) for d in range(1, NY)]
    for dx in range(1, NX):
        far_sent[dx - 1].wait_recv()
        at = -dx % NX * NC
        expand_sibling.append(send(expand_x.at[at, far], expand_x.at[at + 1, far], in_plane(0, 1)))
    next(mig_steps)
    from_z = pick({d: d for d in range(NZ)}, (2 * NZ - z_offset - carry) % NZ)
    arrived_ref[2] = mig_z[from_z]
    for k, copy in enumerate(straight):
        copy.wait_recv()
        arrived_ref[k] = mig_in[k]
    for copy in expand_sibling:
        copy.wait_recv()
    expands = []
    for b in range(BLOCKS):
        oz, ow = stored[b] // PLANE, stored[b] % PLANE
        at = (ow // NC - x + NX) % NX * NC + (ow % NC - c + NC) % NC
        expands.append(expand_x[at, pick(EXPAND_AT, (oz - z + NZ) % NZ)])
    for copy in over_y:
        copy.wait_recv()
    shrink = jnp.sum(part_y[...], axis=0).astype(BF16)
    rows = ROWS // BLOCKS
    lane16 = lanes((rows, HD))
    deltas = [None] * BLOCKS
    for k in range(2):
        mine = shrink[k * rows : (k + 1) * rows].astype(F32)
        left = jnp.where(lane16 < RANK, mine, 0.0)
        right = jnp.where(lane16 < RANK, 0.0, mine)
        both = jnp.concatenate([expands[k], expands[k + 2]], axis=0)
        out = jnp.dot(jnp.concatenate([left, right], axis=0).astype(BF16), both, preferred_element_type=F32)
        deltas[k], deltas[k + 2] = out[:rows], out[rows:]
    fresh_ref[...] = (base + jnp.concatenate(deltas, axis=0)).astype(BF16)

    for copy in copies:
        copy.wait_send()


def attend_kernel(q_ref, draft_ref, keys_ref, values_ref, length_ref, arrived_ref, fresh_ref, out_ref, ko_ref, vo_ref):
    group = q_ref.shape[2] // HD
    heads = group * STEPS
    spot = lax.broadcasted_iota(jnp.int32, (CACHE, HD), 0).astype(F32)
    landing = [arrived_ref[a, 2 * CACHE : 2 * CACHE + 1, :].astype(F32) for a in range(3)]
    lengths = [arrived_ref[a, 2 * CACHE + 1 : 2 * CACHE + 2, :].astype(F32) for a in range(3)]
    fresh = fresh_ref[...].astype(F32)
    lane = lanes((1, HD))
    row_at = lax.broadcasted_iota(jnp.int32, (2 * heads, HD), 0)
    lane_at = lanes((2 * heads, HD))
    same = (row_at // heads) == (lane_at // CACHE)
    ahead = (lane_at % CACHE - row_at % STEPS).astype(F32)
    scale = 1.0 / math.sqrt(HD)

    for pair in range(SLOTS // 2):
        filled, queries = [], []
        for s in (2 * pair, 2 * pair + 1):
            here = [landing[a] == float(s) for a in range(3)]
            fill = jnp.full((1, HD), length_ref[s].astype(F32))
            key, value = keys_ref[s].astype(F32), values_ref[s].astype(F32)
            for a in range(3):
                fill = jnp.where(here[a], lengths[a], fill)
                key = jnp.where(here[a], arrived_ref[a, :CACHE].astype(F32), key)
                value = jnp.where(here[a], arrived_ref[a, CACHE : 2 * CACHE].astype(F32), value)
            after = spot - fill
            draft = draft_ref[s].astype(F32)
            for j in range(STEPS):
                key = jnp.where(after == float(j), draft[j : j + 1], key)
                value = jnp.where(after == float(j), fresh[s * STEPS + j : s * STEPS + j + 1], value)
            ko_ref[s] = key.astype(BF16)
            vo_ref[s] = value.astype(BF16)
            filled.append(fill)
            query = q_ref[s].astype(F32)
            queries += [query[:, g * HD : (g + 1) * HD] for g in range(group)]
        stacked = jnp.concatenate(queries, axis=0).astype(BF16)
        both_keys = ko_ref[2 * pair : 2 * pair + 2].reshape(2 * CACHE, HD)
        both_values = vo_ref[2 * pair : 2 * pair + 2].reshape(2 * CACHE, HD)
        scores = lax.dot_general(stacked, both_keys, (((1,), (1,)), ((), ())), preferred_element_type=F32) * scale
        allowed = same & (ahead <= jnp.where(lane < CACHE, filled[0], filled[1]))
        masked = jnp.where(allowed, scores, -1e30)
        top = jnp.max(masked, axis=-1, keepdims=True)
        raised = jnp.where(allowed, jnp.exp(masked - top), 0.0)
        weights = (raised / jnp.sum(raised, axis=-1, keepdims=True)).astype(BF16)
        attended = jnp.dot(weights, both_values, preferred_element_type=F32)
        for k in range(2):
            for g in range(group):
                at = k * heads + g * STEPS
                out_ref[2 * pair + k, :, g * HD : (g + 1) * HD] = attended[at : at + STEPS].astype(BF16)


def body(
    tokens,
    value_matrix,
    queries,
    draft_keys,
    key_cache_before,
    value_cache_before,
    cache_length,
    migrations,
    block_adapter_index,
    adapter_replica,
    adapter_shrink,
    adapter_expand,
):
    vmem = pl.BlockSpec(memory_space=pltpu.VMEM)
    smem = pl.BlockSpec(memory_space=pltpu.SMEM)
    fresh, arrived = pl.pallas_call(
        comm_kernel,
        out_shape=(
            jax.ShapeDtypeStruct((ROWS, HD), BF16),
            jax.ShapeDtypeStruct((3, MIG_ROWS, HD), BF16),
        ),
        in_specs=[vmem, pl.BlockSpec(memory_space=pl.ANY), vmem, vmem, smem, smem, smem, smem, vmem, vmem],
        out_specs=(vmem, vmem),
        scratch_shapes=[
            pltpu.VMEM(value_matrix.shape, BF16),
            pltpu.SemaphoreType.DMA,
            pltpu.VMEM((ROWS, PART), F32),
            pltpu.VMEM((NY, ROWS, PART), BF16),
            pltpu.VMEM((PLANE, ROWS, PART + HD), BF16),
            pltpu.VMEM((NZ, RANK, PART), BF16),
            pltpu.VMEM((PLANE, NZ, RANK, HD), BF16),
            pltpu.VMEM((3, MIG_ROWS, HD), BF16),
            pltpu.VMEM((2, MIG_ROWS, HD), BF16),
            pltpu.VMEM((PLANE, MIG_ROWS, HD), BF16),
            pltpu.VMEM((NZ, MIG_ROWS, HD), BF16),
            pltpu.VMEM((PLANE * ROWS, HD), F32),
            pltpu.VMEM((PLANE, HALF, HD), F32),
            pltpu.VMEM((PLANE, HALF, HD), F32),
            pltpu.VMEM((NY, HALF, HD), F32),
            pltpu.SemaphoreType.DMA((COPIES,)),
            pltpu.SemaphoreType.DMA((COPIES,)),
        ],
        compiler_params=pltpu.CompilerParams(
            collective_id=0, has_side_effects=True, vmem_limit_bytes=48 * 1024 * 1024
        ),
        name="gather_and_project",
    )(
        tokens,
        value_matrix,
        key_cache_before,
        value_cache_before,
        cache_length,
        migrations,
        block_adapter_index,
        adapter_replica,
        jnp.swapaxes(adapter_shrink[0], 0, 1),
        adapter_expand,
    )
    return pl.pallas_call(
        attend_kernel,
        out_shape=(
            jax.ShapeDtypeStruct(queries.shape, BF16),
            jax.ShapeDtypeStruct(key_cache_before.shape, BF16),
            jax.ShapeDtypeStruct(value_cache_before.shape, BF16),
        ),
        in_specs=[vmem, vmem, vmem, vmem, smem, vmem, vmem],
        out_specs=(vmem, vmem, vmem),
        compiler_params=pltpu.CompilerParams(vmem_limit_bytes=48 * 1024 * 1024),
        name="place_and_attend",
    )(queries, draft_keys, key_cache_before, value_cache_before, cache_length, arrived, fresh)


def solution(mesh):
    placed = (
        P("replica", None, "tensor"),
        P(None, "tensor"),
        P("replica", None, "tensor"),
        P("replica", None, "tensor"),
        P("replica", None, "tensor"),
        P("replica", None, "tensor"),
        P("replica"),
        P("replica", None, None),
        P("replica", None),
        P(),
        P("replica", "tensor", None),
        P("replica", None, "tensor"),
    )
    return jax.shard_map(
        body,
        mesh=mesh,
        in_specs=placed,
        out_specs=(
            P("replica", None, "tensor"),
            P("replica", None, "tensor"),
            P("replica", None, "tensor"),
        ),
        check_vma=False,
    )
```

```python
import math

import jax
import jax.numpy as jnp
from jax import lax
from jax.experimental import pallas as pl
from jax.experimental.pallas import tpu as pltpu
from jax.sharding import PartitionSpec as P

NZ, NX, NC, NY = 8, 4, 2, 8
PLANE = NX * NC
REPLICAS = NZ * PLANE
MESH = pl.DeviceIdType.MESH
F32, BF16 = jnp.float32, jnp.bfloat16

SLOTS, STEPS, BLOCKS, CACHE, HD, RANK = 16, 4, 4, 64, 128, 64
ROWS = SLOTS * STEPS
PART = 1024
HALF = ROWS // 2
MIG_ROWS = 2 * CACHE + 16
COPIES = 128

SHRINK_AT = {1: 0, 7: 1, 2: 2, 6: 3, 3: 4, 5: 5, 0: 6, 4: 7}
EXPAND_AT = {1: 0, 7: 1, 2: 2, 6: 3, 0: 4, 3: 5, 5: 6, 4: 7}
NEAR = 5


def pick(table, index):
    out = jnp.int32(table[0])
    for key, value in table.items():
        if key:
            out = jnp.where(index == key, jnp.int32(value), out)
    return out


def lanes(shape):
    return lax.broadcasted_iota(jnp.int32, shape, len(shape) - 1)


def comm_kernel(
    tok_hbm, w_hbm, keys_hbm, values_hbm, length_hbm, mig_hbm, index_hbm, owner_hbm, shrink_hbm, expand_hbm,
    fresh_ref, arrived_ref,
    tok_ref, w_ref, keys_ref, values_ref, length_ref, mig_ref, index_ref, owner_ref, load_sem, tok_f32,
    tok_y, tok_x, shrink_z, expand_x, mig_out, mig_in, mig_x, mig_z,
    acc, part_out, part_x, part_y, send_sem, recv_sem,
):
    r, t = lax.axis_index("replica"), lax.axis_index("tensor")
    z, w = r // PLANE, r % PLANE
    x, c = w // NC, w % NC

    def along_z(d):
        return ((r + d * PLANE) % REPLICAS, t)

    def along_y(d):
        return (r, (t + d) % NY)

    def in_plane(dx, dc):
        return (z * PLANE + ((x + dx) % NX) * NC + (c + dc) % NC, t)

    sibling = in_plane(0, 1)
    copies = []

    def send(src, dst, device):
        k = len(copies)
        copy = pltpu.make_async_remote_copy(
            src_ref=src, dst_ref=dst, send_sem=send_sem.at[k], recv_sem=recv_sem.at[k],
            device_id=device, device_id_type=MESH,
        )
        copies.append(copy)
        copy.start()
        return copy

    barrier = pltpu.get_barrier_semaphore()
    others = [along_z(1), along_z(-1), along_z(NZ // 2)]
    others += [along_y(d) for d in range(1, NY)]
    others += [in_plane(dx, dc) for dx in range(NX) for dc in range(NC) if dx or dc]
    others += [((r + 1) % REPLICAS, t), ((r + REPLICAS - 1) % REPLICAS, t)]
    for other in others:
        pl.semaphore_signal(barrier, inc=1, device_id=other, device_id_type=MESH)

    loads = [
        pltpu.make_async_copy(src, dst, load_sem.at[k])
        for k, (src, dst) in enumerate([
            (tok_hbm, tok_ref),
            (index_hbm, index_ref),
            (owner_hbm, owner_ref),
            (mig_hbm, mig_ref),
            (length_hbm, length_ref),
            (keys_hbm, keys_ref),
            (values_hbm, values_ref),
            (shrink_hbm, shrink_z.at[SHRINK_AT[0]]),
            (expand_hbm.at[0], expand_x.at[0, EXPAND_AT[0]]),
            (w_hbm, w_ref),
        ])
    ]
    for load in loads:
        load.start()
    tok_loads, mig_loads, late_loads = loads[:3], loads[3:7], loads[7:]

    def ring(n, right, left, parts, split):
        gone = {}
        for k in range(1, n // 2 + 1):
            stay = []
            for h, (at, last) in enumerate(zip(parts, split)):
                for way, device in ((-1, right), (1, left)):
                    if k == n // 2 and last != way:
                        stay.append(gone[k - 1, h, way])
                        continue
                    if k > 1:
                        gone[k - 1, h, way].wait_recv()
                    src, dst = way * (k - 1) % n, way * k % n
                    gone[k, h, way] = send(at(src, k == 1), at(dst, False), device)
            for copy in stay:
                copy.wait_recv()
            yield k - 1
        for (k, _, _), copy in gone.items():
            if k == n // 2:
                copy.wait_recv()
        yield n // 2

    def finish(steps):
        for _ in steps:
            pass

    first_rows, last_rows = pl.ds(0, HALF), pl.ds(HALF, HALF)

    def shrink_part(rows):
        return lambda d, own: shrink_hbm.at[rows] if own else shrink_z.at[SHRINK_AT[d], rows]

    z_steps = ring(
        NZ, along_z(1), along_z(-1),
        [
            lambda d, own: expand_hbm.at[0] if own else expand_x.at[0, EXPAND_AT[d]],
            shrink_part(first_rows),
            shrink_part(last_rows),
        ],
        [-1, -1, 1],
    )
    y_steps = ring(
        NY, along_y(1), along_y(-1),
        [lambda d, own: tok_y.at[d, first_rows], lambda d, own: tok_y.at[d, last_rows]],
        [-1, 1],
    )

    def x_ring(parts):
        return ring(NX, in_plane(1, 0), in_plane(-1, 0), parts, [-1, 1])

    x_steps = x_ring(
        [lambda d, own: tok_x.at[d * NC, first_rows], lambda d, own: tok_x.at[d * NC, last_rows]]
    )
    mig_halves = pl.ds(0, CACHE), pl.ds(CACHE, MIG_ROWS - CACHE)
    mig_x_steps = x_ring(
        [lambda d, own: mig_x.at[d * NC, mig_halves[0]], lambda d, own: mig_x.at[d * NC, mig_halves[1]]]
    )
    mig_steps = ring(
        NZ, along_z(1), along_z(-1),
        [lambda d, own: mig_z.at[d, mig_halves[0]], lambda d, own: mig_z.at[d, mig_halves[1]]],
        [-1, 1],
    )

    def expand_ring(first, middle, last):
        early, late = pl.ds(first, middle - first), pl.ds(middle, last - middle)
        return x_ring([lambda d, own: expand_x.at[d * NC, early], lambda d, own: expand_x.at[d * NC, late]])

    near_steps = expand_ring(0, 3, NEAR)
    far_steps = expand_ring(NEAR, NZ - 1, NZ)

    def to_sibling(at):
        return lambda d: send(at(d * NC), at(d * NC + 1), sibling)

    tokens_over = to_sibling(lambda at: tok_x.at[at])
    mig_over = to_sibling(lambda at: mig_x.at[at])
    near_over = to_sibling(lambda at: expand_x.at[at, pl.ds(0, NEAR)])
    far_over = to_sibling(lambda at: expand_x.at[at, pl.ds(NEAR, NZ - NEAR)])

    base = None

    def add_base(d):
        nonlocal base
        rows = pl.multiple_of((t + d) % NY * PART, PART)
        term = jnp.dot(tok_y[d], w_ref[pl.ds(rows, PART), :], preferred_element_type=F32)
        base = term if base is None else base + term

    pl.semaphore_wait(barrier, len(others))
    next(z_steps)

    for load in tok_loads:
        load.wait()
    for s in range(SLOTS):
        tok_f32[s * STEPS : (s + 1) * STEPS, :] = tok_ref[s].astype(F32)
    own = tok_f32[...].astype(BF16)
    tok_y[0] = own
    next(y_steps)
    tok_x[0, :, 0:PART] = own
    row = lax.broadcasted_iota(jnp.int32, (ROWS, HD), 0)
    stored = [owner_ref[index_ref[0, b]] for b in range(BLOCKS)]
    stored_rows = jnp.zeros((ROWS, HD), F32)
    for b in range(BLOCKS):
        stored_rows = jnp.where(row // (ROWS // BLOCKS) == b, stored[b].astype(F32), stored_rows)
    tok_x[0, :, PART:] = stored_rows.astype(BF16)
    next(x_steps)
    tokens_sent = [tokens_over(0)]

    for load in mig_loads:
        load.wait()
    offsets = [(mig_ref[e, 0, 1] - r + REPLICAS) % REPLICAS for e in range(3)]
    half = REPLICAS // 2
    fits = [
        [o == 1 for o in offsets],
        [o == half for o in offsets],
        [(o != 1) & (o != half) for o in offsets],
    ]

    def chosen(which, column):
        first, second, third = (column(e) for e in range(3))
        return jnp.where(fits[which][0], first, jnp.where(fits[which][1], second, third))

    other_offset = chosen(2, lambda e: offsets[e])
    mig_row = lax.broadcasted_iota(jnp.int32, (16, HD), 0)
    for which in range(3):
        slot = chosen(which, lambda e: mig_ref[e, 0, 0])
        landing = chosen(which, lambda e: mig_ref[e, 0, 2]).astype(F32)
        filled = length_ref[slot].astype(F32)
        notes = jnp.where(mig_row == 0, landing, filled).astype(BF16)
        out = mig_x.at[0] if which == 2 else mig_out.at[which]
        out[0:CACHE] = keys_ref[slot]
        out[CACHE : 2 * CACHE] = values_ref[slot]
        out[2 * CACHE :] = notes
    next(mig_x_steps)
    mig_sent = [mig_over(0)]
    straight = [send(mig_out.at[0], mig_in.at[0], ((r + 1) % REPLICAS, t))]
    for load in late_loads:
        load.wait()
    add_base(0)

    next(z_steps)
    next(y_steps)
    next(x_steps)
    next(mig_x_steps)
    tokens_sent += [tokens_over(1), tokens_over(NX - 1)]
    mig_sent += [mig_over(1), mig_over(NX - 1)]
    add_base(1)
    add_base(NY - 1)
    finish(x_steps)
    tokens_sent += [tokens_over(2)]
    finish(mig_x_steps)
    mig_sent += [mig_over(2)]

    next(z_steps)
    next(y_steps)
    next(near_steps)
    near_sent = [near_over(0)]

    for copy in mig_sent:
        copy.wait_recv()
    plane_offset, z_offset = other_offset % PLANE, other_offset // PLANE
    from_w = (w - plane_offset + PLANE) % PLANE
    carry = jnp.where(from_w + plane_offset >= PLANE, 1, 0)
    from_slot = (from_w // NC - x + NX) % NX * NC + (from_w % NC - c + NC) % NC
    mig_z[0] = mig_x[from_slot]

    for copy in tokens_sent:
        copy.wait_recv()
    lane = lanes((1, HD))
    stored_all = tok_x[:, :, PART:].reshape(PLANE * ROWS, HD).astype(F32)

    def add_products(pair, pairs):
        some = shrink_z[2 * pair : 2 * (pair + pairs)].reshape(2 * pairs * RANK, PART)
        product = lax.dot_general(
            tok_x[:, :, 0:PART].reshape(PLANE * ROWS, PART), some, (((1,), (1,)), ((), ())),
            preferred_element_type=F32,
        )
        out = None if pair == 0 else acc[...]
        for k in range(pairs):
            first, second = (
                ((r + d * PLANE) % REPLICAS).astype(F32) for d, at in SHRINK_AT.items() if at // 2 == pair + k
            )
            mine = stored_all == jnp.where(lane < RANK, first, second)
            term = jnp.where(mine, product[:, k * HD : (k + 1) * HD], 0.0)
            out = term if out is None else out + term
        return out

    acc[...] = add_products(0, 2)

    next(z_steps)
    next(y_steps)
    straight += [send(mig_out.at[1], mig_in.at[1], along_z(half // PLANE))]
    next(mig_steps)
    next(near_steps)
    near_sent += [near_over(1), near_over(NX - 1)]
    acc[...] = add_products(2, 1)
    add_base(2)
    add_base(NY - 2)
    next(mig_steps)
    next(z_steps)
    next(far_steps)
    far_sent = [far_over(0)]

    total = add_products(3, 1).reshape(PLANE, ROWS, HD)
    total = total + jnp.concatenate([total[:, :, RANK:], total[:, :, :RANK]], axis=-1)
    total = jnp.where(lanes((PLANE, HALF, HD)) < RANK, total[:, :HALF], total[:, HALF:])
    part_out[...] = total.astype(BF16)
    part_sent = []
    for dx in range(NX):
        for dc in range(NC):
            if dx or dc:
                back = (-dx % NX) * NC + dc
                part_sent.append(send(part_out.at[dx * NC + dc], part_x.at[back], in_plane(dx, dc)))
    part_x[0] = part_out[0]
    finish(near_steps)
    near_sent += [near_over(2)]
    next(far_steps)
    far_sent += [far_over(1), far_over(NX - 1)]
    for copy in part_sent:
        copy.wait_recv()
    part_y[0] = jnp.sum(part_x[...].astype(F32), axis=0).astype(BF16)
    over_y = [send(part_y.at[0], part_y.at[NY - d], along_y(d)) for d in range(1, NY)]
    add_base(3)
    add_base(NY - 3)
    next(y_steps)
    add_base(4)
    finish(far_steps)
    far_sent += [far_over(2)]
    next(mig_steps)
    next(mig_steps)
    next(mig_steps)
    from_z = (2 * NZ - z_offset - carry) % NZ
    arrived_ref[2] = mig_z[from_z]
    for k, copy in enumerate(straight):
        copy.wait_recv()
        arrived_ref[k] = mig_in[k]
    for copy in near_sent + far_sent:
        copy.wait_recv()
    expands = []
    for b in range(BLOCKS):
        oz, ow = stored[b] // PLANE, stored[b] % PLANE
        at = (ow // NC - x + NX) % NX * NC + (ow % NC - c + NC) % NC
        expands.append(expand_x[at, pick(EXPAND_AT, (oz - z + NZ) % NZ)])
    for copy in over_y:
        copy.wait_recv()
    shrink = jnp.sum(part_y[...].astype(F32), axis=0).astype(BF16)
    rows = ROWS // BLOCKS
    lane16 = lanes((rows, HD))
    deltas = [None] * BLOCKS
    for k in range(2):
        mine = shrink[k * rows : (k + 1) * rows].astype(F32)
        left = jnp.where(lane16 < RANK, mine, 0.0)
        right = jnp.where(lane16 < RANK, 0.0, mine)
        both = jnp.concatenate([expands[k], expands[k + 2]], axis=0)
        out = jnp.dot(jnp.concatenate([left, right], axis=0).astype(BF16), both, preferred_element_type=F32)
        deltas[k], deltas[k + 2] = out[:rows], out[rows:]
    fresh_ref[...] = (base + jnp.concatenate(deltas, axis=0)).astype(BF16)

    for copy in copies:
        copy.wait_send()


def attend_kernel(
    q_ref, draft_ref, keys_ref, values_ref, length_ref, arrived_ref, fresh_ref,
    out_hbm, ko_hbm, vo_hbm, out_ref, ko_ref, vo_ref, sem,
):
    group = q_ref.shape[2] // HD
    heads = group * STEPS
    spot = lax.broadcasted_iota(jnp.int32, (CACHE, HD), 0).astype(F32)
    landing = [arrived_ref[a, 2 * CACHE : 2 * CACHE + 1, :].astype(F32) for a in range(3)]
    lengths = [arrived_ref[a, 2 * CACHE + 1 : 2 * CACHE + 2, :].astype(F32) for a in range(3)]
    lane = lanes((1, HD))
    row_at = lax.broadcasted_iota(jnp.int32, (2 * heads, HD), 0)
    lane_at = lanes((2 * heads, HD))
    same = (row_at // heads) == (lane_at // CACHE)
    ahead = (lane_at % CACHE - row_at % STEPS).astype(F32)
    scale = 1.0 / math.sqrt(HD)
    pairs = range(SLOTS // 2)

    filled = []
    for s in range(SLOTS):
        fill = jnp.full((1, HD), length_ref[s].astype(F32))
        for a in range(3):
            fill = jnp.where(landing[a] == float(s), lengths[a], fill)
        filled.append(fill)

    def place(old_ref, first_row, new, out):
        for s in range(SLOTS):
            held = old_ref[s].astype(F32)
            for a in range(3):
                came = arrived_ref[a, first_row : first_row + CACHE].astype(F32)
                held = jnp.where(landing[a] == float(s), came, held)
            after = spot - filled[s]
            rows = new(s)
            for j in range(STEPS):
                held = jnp.where(after == float(j), rows[j : j + 1], held)
            out[s] = held.astype(BF16)

    place(keys_ref, 0, lambda s: draft_ref[s].astype(F32), ko_ref)
    keys_gone = pltpu.make_async_copy(ko_ref, ko_hbm, sem.at[0])
    keys_gone.start()
    scores = []
    for pair in pairs:
        queries = []
        for s in (2 * pair, 2 * pair + 1):
            query = q_ref[s].astype(F32)
            queries += [query[:, g * HD : (g + 1) * HD] for g in range(group)]
        stacked = jnp.concatenate(queries, axis=0).astype(BF16)
        both = ko_ref[2 * pair : 2 * pair + 2].reshape(2 * CACHE, HD)
        scores.append(lax.dot_general(stacked, both, (((1,), (1,)), ((), ())), preferred_element_type=F32) * scale)
    place(values_ref, CACHE, lambda s: fresh_ref[s * STEPS : (s + 1) * STEPS].astype(F32), vo_ref)
    values_gone = pltpu.make_async_copy(vo_ref, vo_hbm, sem.at[1])
    values_gone.start()
    weights = []
    for pair in pairs:
        allowed = same & (ahead <= jnp.where(lane < CACHE, filled[2 * pair], filled[2 * pair + 1]))
        masked = jnp.where(allowed, scores[pair], -1e30)
        top = jnp.max(masked, axis=-1, keepdims=True)
        raised = jnp.where(allowed, jnp.exp(masked - top), 0.0)
        weights.append((raised / jnp.sum(raised, axis=-1, keepdims=True)).astype(BF16))
    for pair in pairs:
        both = vo_ref[2 * pair : 2 * pair + 2].reshape(2 * CACHE, HD)
        attended = jnp.dot(weights[pair], both, preferred_element_type=F32)
        for k in range(2):
            for g in range(group):
                at = k * heads + g * STEPS
                out_ref[2 * pair + k, :, g * HD : (g + 1) * HD] = attended[at : at + STEPS].astype(BF16)
    out_gone = pltpu.make_async_copy(out_ref, out_hbm, sem.at[2])
    out_gone.start()
    keys_gone.wait()
    values_gone.wait()
    out_gone.wait()


def body(
    tokens,
    value_matrix,
    queries,
    draft_keys,
    key_cache_before,
    value_cache_before,
    cache_length,
    migrations,
    block_adapter_index,
    adapter_replica,
    adapter_shrink,
    adapter_expand,
):
    vmem = pl.BlockSpec(memory_space=pltpu.VMEM)
    hbm = pl.BlockSpec(memory_space=pltpu.HBM)
    smem = pl.BlockSpec(memory_space=pltpu.SMEM)
    fresh, arrived = pl.pallas_call(
        comm_kernel,
        out_shape=(
            jax.ShapeDtypeStruct((ROWS, HD), BF16),
            jax.ShapeDtypeStruct((3, MIG_ROWS, HD), BF16),
        ),
        in_specs=[hbm] * 10,
        out_specs=(vmem, vmem),
        scratch_shapes=[
            pltpu.VMEM(tokens.shape, BF16),
            pltpu.VMEM(value_matrix.shape, BF16),
            pltpu.VMEM(key_cache_before.shape, BF16),
            pltpu.VMEM(value_cache_before.shape, BF16),
            pltpu.SMEM(cache_length.shape, jnp.int32),
            pltpu.SMEM((3, 1, 3), jnp.int32),
            pltpu.SMEM(block_adapter_index.shape, jnp.int32),
            pltpu.SMEM(adapter_replica.shape, jnp.int32),
            pltpu.SemaphoreType.DMA((10,)),
            pltpu.VMEM((ROWS, PART), F32),
            pltpu.VMEM((NY, ROWS, PART), BF16),
            pltpu.VMEM((PLANE, ROWS, PART + HD), BF16),
            pltpu.VMEM((NZ, RANK, PART), BF16),
            pltpu.VMEM((PLANE, NZ, RANK, HD), BF16),
            pltpu.VMEM((2, MIG_ROWS, HD), BF16),
            pltpu.VMEM((2, MIG_ROWS, HD), BF16),
            pltpu.VMEM((PLANE, MIG_ROWS, HD), BF16),
            pltpu.VMEM((NZ, MIG_ROWS, HD), BF16),
            pltpu.VMEM((PLANE * ROWS, HD), F32),
            pltpu.VMEM((PLANE, HALF, HD), BF16),
            pltpu.VMEM((PLANE, HALF, HD), BF16),
            pltpu.VMEM((NY, HALF, HD), BF16),
            pltpu.SemaphoreType.DMA((COPIES,)),
            pltpu.SemaphoreType.DMA((COPIES,)),
        ],
        compiler_params=pltpu.CompilerParams(
            collective_id=0, has_side_effects=True, vmem_limit_bytes=32 * 1024 * 1024
        ),
        name="gather_and_project",
    )(
        *(
            pltpu.with_memory_space_constraint(operand, pltpu.HBM)
            for operand in (
                tokens,
                value_matrix,
                key_cache_before,
                value_cache_before,
                cache_length,
                jnp.transpose(migrations, (1, 0, 2)),
                block_adapter_index,
                adapter_replica,
                jnp.swapaxes(adapter_shrink[0], 0, 1),
                adapter_expand,
            )
        )
    )
    return pl.pallas_call(
        attend_kernel,
        out_shape=(
            jax.ShapeDtypeStruct(queries.shape, BF16),
            jax.ShapeDtypeStruct(key_cache_before.shape, BF16),
            jax.ShapeDtypeStruct(value_cache_before.shape, BF16),
        ),
        in_specs=[vmem, vmem, vmem, vmem, smem, vmem, vmem],
        out_specs=(hbm, hbm, hbm),
        scratch_shapes=[
            pltpu.VMEM(queries.shape, BF16),
            pltpu.VMEM(key_cache_before.shape, BF16),
            pltpu.VMEM(value_cache_before.shape, BF16),
            pltpu.SemaphoreType.DMA((3,)),
        ],
        compiler_params=pltpu.CompilerParams(vmem_limit_bytes=24 * 1024 * 1024),
        name="place_and_attend",
    )(queries, draft_keys, key_cache_before, value_cache_before, cache_length, arrived, fresh)


def solution(mesh):
    placed = (
        P("replica", None, "tensor"),
        P(None, "tensor"),
        P("replica", None, "tensor"),
        P("replica", None, "tensor"),
        P("replica", None, "tensor"),
        P("replica", None, "tensor"),
        P("replica"),
        P("replica", None, None),
        P("replica", None),
        P(),
        P("replica", "tensor", None),
        P("replica", None, "tensor"),
    )
    return jax.shard_map(
        body,
        mesh=mesh,
        in_specs=placed,
        out_specs=(
            P("replica", None, "tensor"),
            P("replica", None, "tensor"),
            P("replica", None, "tensor"),
        ),
        check_vma=False,
    )
```

```python
import itertools
import math

import jax
import jax.numpy as jnp
from jax import lax
from jax.experimental import pallas as pl
from jax.experimental.pallas import tpu as pltpu
from jax.sharding import PartitionSpec as P

NZ, NX, NC, NY = 8, 4, 2, 8
PLANE = NX * NC
REPLICAS = NZ * PLANE
MESH = pl.DeviceIdType.MESH
F32, BF16 = jnp.float32, jnp.bfloat16

SLOTS, STEPS, BLOCKS, CACHE, HD, RANK = 16, 4, 4, 64, 128, 64
ROWS = SLOTS * STEPS
PART = 1024
HALF = ROWS // 2
MIG_ROWS = 2 * CACHE + 16
COPIES = 136

SHRINK_AT = {1: 0, 7: 1, 2: 2, 6: 3, 3: 4, 5: 5, 0: 6, 4: 7}
EXPAND_AT = {1: 0, 7: 1, 2: 2, 6: 3, 0: 4, 3: 5, 5: 6, 4: 7}
NEAR = 5


def pick(table, index):
    out = jnp.int32(table[0])
    for key, value in table.items():
        if key:
            out = jnp.where(index == key, jnp.int32(value), out)
    return out


def lanes(shape):
    return lax.broadcasted_iota(jnp.int32, shape, len(shape) - 1)


def comm_kernel(
    tok_hbm, w_hbm, keys_hbm, values_hbm, length_hbm, mig_hbm, index_hbm, owner_hbm, shrink_hbm, expand_hbm,
    fresh_ref, arrived_ref,
    tok_ref, w_ref, keys_ref, values_ref, length_ref, mig_ref, index_ref, owner_ref, load_sem, tok_f32,
    tok_y, tok_x, shrink_z, expand_x, mig_out, mig_in, mig_x, mig_z,
    acc, part_out, part_x, part_y, send_sem, recv_sem,
):
    r, t = lax.axis_index("replica"), lax.axis_index("tensor")
    z, w = r // PLANE, r % PLANE
    x, c = w // NC, w % NC

    def along_z(d):
        return ((r + d * PLANE) % REPLICAS, t)

    def along_y(d):
        return (r, (t + d) % NY)

    def in_plane(dx, dc):
        return (z * PLANE + ((x + dx) % NX) * NC + (c + dc) % NC, t)

    sibling = in_plane(0, 1)
    copies, numbers = [], itertools.count()

    def send(src, dst, device):
        k = next(numbers)
        copy = pltpu.make_async_remote_copy(
            src_ref=src, dst_ref=dst, send_sem=send_sem.at[k], recv_sem=recv_sem.at[k],
            device_id=device, device_id_type=MESH,
        )
        copies.append(copy)
        copy.start()
        return copy

    barrier = pltpu.get_barrier_semaphore()
    others = [along_z(1), along_z(-1), along_z(NZ // 2)]
    others += [along_y(d) for d in range(1, NY)]
    others += [in_plane(dx, dc) for dx in range(NX) for dc in range(NC) if dx or dc]
    others += [((r + 1) % REPLICAS, t), ((r + REPLICAS - 1) % REPLICAS, t)]
    for other in others:
        pl.semaphore_signal(barrier, inc=1, device_id=other, device_id_type=MESH)

    loads = [
        pltpu.make_async_copy(src, dst, load_sem.at[k])
        for k, (src, dst) in enumerate([
            (tok_hbm, tok_ref),
            (index_hbm, index_ref),
            (owner_hbm, owner_ref),
            (mig_hbm, mig_ref),
            (length_hbm, length_ref),
            (keys_hbm, keys_ref),
            (values_hbm, values_ref),
            (shrink_hbm, shrink_z.at[SHRINK_AT[0]]),
            (expand_hbm.at[0], expand_x.at[0, EXPAND_AT[0]]),
            (w_hbm, w_ref),
        ])
    ]
    load_w = loads.pop()
    for load in loads:
        load.start()
    tok_loads, mig_loads, late_loads = loads[:3], loads[3:7], loads[7:]

    def ring(n, right, left, groups):
        gone = {}
        for k in range(1, n // 2 + 1):
            for h, views in enumerate(groups):
                ways = {-1: right, 1: left}
                stays = []
                if k == n // 2:
                    stays = [1 if 2 * h < len(groups) else -1]
                    del ways[stays[0]]
                for v, at in enumerate(views):
                    for way, device in ways.items():
                        if k > 1:
                            gone[k - 1, h, v, way].wait_recv()
                        src, dst = way * (k - 1) % n, way * k % n
                        gone[k, h, v, way] = send(at(src, k == 1), at(dst, False), device)
                for v in range(len(views)):
                    for way in stays:
                        gone[k - 1, h, v, way].wait_recv()
                yield k, h
        for (k, *_), copy in gone.items():
            if k == n // 2:
                copy.wait_recv()
        yield n, 0

    def last(steps, n):
        for _ in range(n):
            next(steps)

    first_rows, last_rows = pl.ds(0, HALF), pl.ds(HALF, HALF)

    def shrink_part(rows):
        return lambda d, own: shrink_hbm.at[rows] if own else shrink_z.at[SHRINK_AT[d], rows]

    z_steps = ring(
        NZ, along_z(1), along_z(-1),
        [
            [lambda d, own: expand_hbm.at[0] if own else expand_x.at[0, EXPAND_AT[d]], shrink_part(pl.ds(0, 16))],
            [shrink_part(pl.ds(16, 16))],
            [shrink_part(pl.ds(32, 16))],
            [shrink_part(pl.ds(48, 16))],
        ],
    )
    y_steps = ring(
        NY, along_y(1), along_y(-1),
        [[lambda d, own: tok_y.at[d, first_rows]], [lambda d, own: tok_y.at[d, last_rows]]],
    )

    def x_ring(first, second):
        return ring(NX, in_plane(1, 0), in_plane(-1, 0), [[first], [second]])

    x_steps = x_ring(
        lambda d, own: tok_x.at[d * NC, first_rows], lambda d, own: tok_x.at[d * NC, last_rows]
    )
    mig_halves = pl.ds(0, CACHE), pl.ds(CACHE, MIG_ROWS - CACHE)
    mig_x_steps = x_ring(
        lambda d, own: mig_x.at[d * NC, mig_halves[0]], lambda d, own: mig_x.at[d * NC, mig_halves[1]]
    )
    mig_steps = ring(
        NZ, along_z(1), along_z(-1),
        [[lambda d, own: mig_z.at[d, mig_halves[0]]], [lambda d, own: mig_z.at[d, mig_halves[1]]]],
    )

    def expand_ring(first, middle, end):
        early, late = pl.ds(first, middle - first), pl.ds(middle, end - middle)
        return x_ring(lambda d, own: expand_x.at[d * NC, early], lambda d, own: expand_x.at[d * NC, late])

    near_steps = expand_ring(0, 3, NEAR)

    def to_plane(src, dst):
        return [
            send(src(dx * NC + dc), dst((-dx % NX) * NC + dc), in_plane(dx, dc))
            for dx in range(NX)
            for dc in range(NC)
            if dx or dc
        ]

    def to_sibling(at):
        return lambda d: send(at(d * NC), at(d * NC + 1), sibling)

    tokens_over = to_sibling(lambda at: tok_x.at[at])
    mig_over = to_sibling(lambda at: mig_x.at[at])
    near_over = to_sibling(lambda at: expand_x.at[at, pl.ds(0, NEAR)])

    base = None

    def add_base(d):
        nonlocal base
        rows = pl.multiple_of((t + d) % NY * PART, PART)
        term = jnp.dot(tok_y[d], w_ref[pl.ds(rows, PART), :], preferred_element_type=F32)
        base = term if base is None else base + term

    pl.semaphore_wait(barrier, len(others))
    last(z_steps, 4)

    for load in tok_loads:
        load.wait()
    for s in range(SLOTS):
        tok_f32[s * STEPS : (s + 1) * STEPS, :] = tok_ref[s].astype(F32)
    own = tok_f32[...].astype(BF16)
    tok_x[0, :, 0:PART] = own
    row = lax.broadcasted_iota(jnp.int32, (ROWS, HD), 0)
    stored = [owner_ref[index_ref[0, b]] for b in range(BLOCKS)]
    stored_rows = jnp.zeros((ROWS, HD), F32)
    for b in range(BLOCKS):
        stored_rows = jnp.where(row // (ROWS // BLOCKS) == b, stored[b].astype(F32), stored_rows)
    tok_x[0, :, PART:] = stored_rows.astype(BF16)
    last(x_steps, 2)
    tokens_sent = [tokens_over(0)]
    tok_y[0] = own
    last(y_steps, 2)
    load_w.start()

    for load in mig_loads:
        load.wait()
    offsets = [(mig_ref[e, 0, 1] - r + REPLICAS) % REPLICAS for e in range(3)]
    half = REPLICAS // 2
    fits = [
        [o == 1 for o in offsets],
        [o == half for o in offsets],
        [(o != 1) & (o != half) for o in offsets],
    ]

    def chosen(which, column):
        first, second, third = (column(e) for e in range(3))
        return jnp.where(fits[which][0], first, jnp.where(fits[which][1], second, third))

    other_offset = chosen(2, lambda e: offsets[e])
    mig_row = lax.broadcasted_iota(jnp.int32, (16, HD), 0)
    for which in range(3):
        slot = chosen(which, lambda e: mig_ref[e, 0, 0])
        landing = chosen(which, lambda e: mig_ref[e, 0, 2]).astype(F32)
        filled = length_ref[slot].astype(F32)
        notes = jnp.where(mig_row == 0, landing, filled).astype(BF16)
        out = mig_x.at[0] if which == 2 else mig_out.at[which]
        out[0:CACHE] = keys_ref[slot]
        out[CACHE : 2 * CACHE] = values_ref[slot]
        out[2 * CACHE :] = notes
    last(mig_x_steps, 2)
    mig_sent = [mig_over(0)]
    straight = [send(mig_out.at[0], mig_in.at[0], ((r + 1) % REPLICAS, t))]
    for load in late_loads:
        load.wait()
    load_w.wait()
    add_base(0)
    last(z_steps, 4)
    last(x_steps, 2)
    tokens_sent += [tokens_over(1), tokens_over(NX - 1)]
    last(mig_x_steps, 2)
    mig_sent += [mig_over(1), mig_over(NX - 1)]
    last(z_steps, 4)
    last(x_steps, 1)
    tokens_sent += [tokens_over(2)]
    last(mig_x_steps, 1)
    mig_sent += [mig_over(2)]
    last(near_steps, 2)
    near_sent = [near_over(0)]
    last(y_steps, 2)
    for copy in tokens_sent:
        copy.wait_recv()
    lane = lanes((1, HD))

    def add_products(pair, pairs):
        some = shrink_z[2 * pair : 2 * (pair + pairs)].reshape(2 * pairs * RANK, PART)
        product = lax.dot_general(
            tok_x[:, :, 0:PART].reshape(PLANE * ROWS, PART), some, (((1,), (1,)), ((), ())),
            preferred_element_type=F32,
        )
        stored_all = tok_x[:, :, PART:].reshape(PLANE * ROWS, HD).astype(F32)
        out = None if pair == 0 else acc[...]
        for k in range(pairs):
            first, second = (
                ((r + d * PLANE) % REPLICAS).astype(F32) for d, at in SHRINK_AT.items() if at // 2 == pair + k
            )
            mine = stored_all == jnp.where(lane < RANK, first, second)
            term = jnp.where(mine, product[:, k * HD : (k + 1) * HD], 0.0)
            out = term if out is None else out + term
        return out

    acc[...] = add_products(0, 2)

    last(z_steps, 4)
    far = pl.ds(NEAR, 2)
    far_sent = to_plane(lambda at: expand_x.at[0, far], lambda at: expand_x.at[at, far])
    for copy in mig_sent:
        copy.wait_recv()
    plane_offset, z_offset = other_offset % PLANE, other_offset // PLANE
    from_w = (w - plane_offset + PLANE) % PLANE
    carry = jnp.where(from_w + plane_offset >= PLANE, 1, 0)
    from_slot = (from_w // NC - x + NX) % NX * NC + (from_w % NC - c + NC) % NC
    mig_z[0] = mig_x[from_slot]
    last(mig_steps, 2)
    last(near_steps, 2)
    near_sent += [near_over(1), near_over(NX - 1)]
    acc[...] = add_products(2, 1)
    last(z_steps, 1)
    far_sent += to_plane(lambda at: expand_x.at[0, NZ - 1], lambda at: expand_x.at[at, NZ - 1])
    last(mig_steps, 2)

    total = add_products(3, 1).reshape(PLANE, ROWS, HD)
    total = total + jnp.concatenate([total[:, :, RANK:], total[:, :, :RANK]], axis=-1)
    total = jnp.where(lanes((PLANE, HALF, HD)) < RANK, total[:, :HALF], total[:, HALF:])
    part_out[...] = total.astype(BF16)
    part_sent = to_plane(lambda at: part_out.at[at], lambda at: part_x.at[at])
    part_x[0] = part_out[0]
    straight += [send(mig_out.at[1], mig_in.at[1], along_z(half // PLANE))]
    last(near_steps, 1)
    near_sent += [near_over(2)]
    last(y_steps, 2)
    add_base(1)
    add_base(NY - 1)
    last(mig_steps, 2)
    for copy in part_sent:
        copy.wait_recv()
    part_y[0] = jnp.sum(part_x[...].astype(F32), axis=0).astype(BF16)
    over_y = [send(part_y.at[0], part_y.at[NY - d], along_y(d)) for d in range(1, NY)]
    last(y_steps, 2)
    last(mig_steps, 2)
    add_base(2)
    add_base(NY - 2)
    add_base(3)
    add_base(NY - 3)
    last(y_steps, 1)
    add_base(4)
    last(mig_steps, 1)
    from_z = (2 * NZ - z_offset - carry) % NZ
    arrived_ref[2] = mig_z[from_z]
    for k, copy in enumerate(straight):
        copy.wait_recv()
        arrived_ref[k] = mig_in[k]
    for copy in near_sent + far_sent:
        copy.wait_recv()
    expands = []
    for b in range(BLOCKS):
        oz, ow = stored[b] // PLANE, stored[b] % PLANE
        at = (ow // NC - x + NX) % NX * NC + (ow % NC - c + NC) % NC
        expands.append(expand_x[at, pick(EXPAND_AT, (oz - z + NZ) % NZ)])
    for copy in over_y:
        copy.wait_recv()
    shrink = jnp.sum(part_y[...].astype(F32), axis=0).astype(BF16)
    rows = ROWS // BLOCKS
    lane16 = lanes((rows, HD))
    deltas = [None] * BLOCKS
    for k in range(2):
        mine = shrink[k * rows : (k + 1) * rows].astype(F32)
        left = jnp.where(lane16 < RANK, mine, 0.0)
        right = jnp.where(lane16 < RANK, 0.0, mine)
        both = jnp.concatenate([expands[k], expands[k + 2]], axis=0)
        out = jnp.dot(jnp.concatenate([left, right], axis=0).astype(BF16), both, preferred_element_type=F32)
        deltas[k], deltas[k + 2] = out[:rows], out[rows:]
    fresh_ref[...] = (base + jnp.concatenate(deltas, axis=0)).astype(BF16)

    for copy in copies:
        copy.wait_send()


def attend_kernel(
    q_ref, draft_ref, keys_ref, values_ref, length_ref, arrived_ref, fresh_ref,
    out_hbm, ko_hbm, vo_hbm, out_ref, ko_ref, vo_ref, sem,
):
    group = q_ref.shape[2] // HD
    heads = group * STEPS
    spot = lax.broadcasted_iota(jnp.int32, (CACHE, HD), 0).astype(F32)
    landing = [arrived_ref[a, 2 * CACHE : 2 * CACHE + 1, :].astype(F32) for a in range(3)]
    lengths = [arrived_ref[a, 2 * CACHE + 1 : 2 * CACHE + 2, :].astype(F32) for a in range(3)]
    lane = lanes((1, HD))
    row_at = lax.broadcasted_iota(jnp.int32, (2 * heads, HD), 0)
    lane_at = lanes((2 * heads, HD))
    same = (row_at // heads) == (lane_at // CACHE)
    ahead = (lane_at % CACHE - row_at % STEPS).astype(F32)
    scale = 1.0 / math.sqrt(HD)
    pairs = range(SLOTS // 2)

    filled = []
    for s in range(SLOTS):
        fill = jnp.full((1, HD), length_ref[s].astype(F32))
        for a in range(3):
            fill = jnp.where(landing[a] == float(s), lengths[a], fill)
        filled.append(fill)

    def place(old_ref, first_row, new, out):
        for s in range(SLOTS):
            held = old_ref[s].astype(F32)
            for a in range(3):
                came = arrived_ref[a, first_row : first_row + CACHE].astype(F32)
                held = jnp.where(landing[a] == float(s), came, held)
            after = spot - filled[s]
            rows = new(s)
            for j in range(STEPS):
                held = jnp.where(after == float(j), rows[j : j + 1], held)
            out[s] = held.astype(BF16)

    place(keys_ref, 0, lambda s: draft_ref[s].astype(F32), ko_ref)
    keys_gone = pltpu.make_async_copy(ko_ref, ko_hbm, sem.at[0])
    keys_gone.start()
    scores = []
    for pair in pairs:
        queries = []
        for s in (2 * pair, 2 * pair + 1):
            query = q_ref[s].astype(F32)
            queries += [query[:, g * HD : (g + 1) * HD] for g in range(group)]
        stacked = jnp.concatenate(queries, axis=0).astype(BF16)
        both = ko_ref[2 * pair : 2 * pair + 2].reshape(2 * CACHE, HD)
        scores.append(lax.dot_general(stacked, both, (((1,), (1,)), ((), ())), preferred_element_type=F32) * scale)
    place(values_ref, CACHE, lambda s: fresh_ref[s * STEPS : (s + 1) * STEPS].astype(F32), vo_ref)
    values_gone = pltpu.make_async_copy(vo_ref, vo_hbm, sem.at[1])
    values_gone.start()
    weights = []
    for pair in pairs:
        allowed = same & (ahead <= jnp.where(lane < CACHE, filled[2 * pair], filled[2 * pair + 1]))
        masked = jnp.where(allowed, scores[pair], -1e30)
        top = jnp.max(masked, axis=-1, keepdims=True)
        raised = jnp.where(allowed, jnp.exp(masked - top), 0.0)
        weights.append((raised / jnp.sum(raised, axis=-1, keepdims=True)).astype(BF16))
    for pair in pairs:
        both = vo_ref[2 * pair : 2 * pair + 2].reshape(2 * CACHE, HD)
        attended = jnp.dot(weights[pair], both, preferred_element_type=F32)
        for k in range(2):
            for g in range(group):
                at = k * heads + g * STEPS
                out_ref[2 * pair + k, :, g * HD : (g + 1) * HD] = attended[at : at + STEPS].astype(BF16)
    out_gone = pltpu.make_async_copy(out_ref, out_hbm, sem.at[2])
    out_gone.start()
    keys_gone.wait()
    values_gone.wait()
    out_gone.wait()


def body(
    tokens,
    value_matrix,
    queries,
    draft_keys,
    key_cache_before,
    value_cache_before,
    cache_length,
    migrations,
    block_adapter_index,
    adapter_replica,
    adapter_shrink,
    adapter_expand,
):
    vmem = pl.BlockSpec(memory_space=pltpu.VMEM)
    hbm = pl.BlockSpec(memory_space=pltpu.HBM)
    smem = pl.BlockSpec(memory_space=pltpu.SMEM)
    fresh, arrived = pl.pallas_call(
        comm_kernel,
        out_shape=(
            jax.ShapeDtypeStruct((ROWS, HD), BF16),
            jax.ShapeDtypeStruct((3, MIG_ROWS, HD), BF16),
        ),
        in_specs=[hbm] * 10,
        out_specs=(vmem, vmem),
        scratch_shapes=[
            pltpu.VMEM(tokens.shape, BF16),
            pltpu.VMEM(value_matrix.shape, BF16),
            pltpu.VMEM(key_cache_before.shape, BF16),
            pltpu.VMEM(value_cache_before.shape, BF16),
            pltpu.SMEM(cache_length.shape, jnp.int32),
            pltpu.SMEM((3, 1, 3), jnp.int32),
            pltpu.SMEM(block_adapter_index.shape, jnp.int32),
            pltpu.SMEM(adapter_replica.shape, jnp.int32),
            pltpu.SemaphoreType.DMA((10,)),
            pltpu.VMEM((ROWS, PART), F32),
            pltpu.VMEM((NY, ROWS, PART), BF16),
            pltpu.VMEM((PLANE, ROWS, PART + HD), BF16),
            pltpu.VMEM((NZ, RANK, PART), BF16),
            pltpu.VMEM((PLANE, NZ, RANK, HD), BF16),
            pltpu.VMEM((2, MIG_ROWS, HD), BF16),
            pltpu.VMEM((2, MIG_ROWS, HD), BF16),
            pltpu.VMEM((PLANE, MIG_ROWS, HD), BF16),
            pltpu.VMEM((NZ, MIG_ROWS, HD), BF16),
            pltpu.VMEM((PLANE * ROWS, HD), F32),
            pltpu.VMEM((PLANE, HALF, HD), BF16),
            pltpu.VMEM((PLANE, HALF, HD), BF16),
            pltpu.VMEM((NY, HALF, HD), BF16),
            pltpu.SemaphoreType.DMA((COPIES,)),
            pltpu.SemaphoreType.DMA((COPIES,)),
        ],
        compiler_params=pltpu.CompilerParams(
            collective_id=0, has_side_effects=True, vmem_limit_bytes=32 * 1024 * 1024
        ),
        name="gather_and_project",
    )(
        *(
            pltpu.with_memory_space_constraint(operand, pltpu.HBM)
            for operand in (
                tokens,
                value_matrix,
                key_cache_before,
                value_cache_before,
                cache_length,
                jnp.transpose(migrations, (1, 0, 2)),
                block_adapter_index,
                adapter_replica,
                jnp.swapaxes(adapter_shrink[0], 0, 1),
                adapter_expand,
            )
        )
    )
    return pl.pallas_call(
        attend_kernel,
        out_shape=(
            jax.ShapeDtypeStruct(queries.shape, BF16),
            jax.ShapeDtypeStruct(key_cache_before.shape, BF16),
            jax.ShapeDtypeStruct(value_cache_before.shape, BF16),
        ),
        in_specs=[vmem, vmem, vmem, vmem, smem, vmem, vmem],
        out_specs=(hbm, hbm, hbm),
        scratch_shapes=[
            pltpu.VMEM(queries.shape, BF16),
            pltpu.VMEM(key_cache_before.shape, BF16),
            pltpu.VMEM(value_cache_before.shape, BF16),
            pltpu.SemaphoreType.DMA((3,)),
        ],
        compiler_params=pltpu.CompilerParams(vmem_limit_bytes=24 * 1024 * 1024),
        name="place_and_attend",
    )(queries, draft_keys, key_cache_before, value_cache_before, cache_length, arrived, fresh)


def solution(mesh):
    placed = (
        P("replica", None, "tensor"),
        P(None, "tensor"),
        P("replica", None, "tensor"),
        P("replica", None, "tensor"),
        P("replica", None, "tensor"),
        P("replica", None, "tensor"),
        P("replica"),
        P("replica", None, None),
        P("replica", None),
        P(),
        P("replica", "tensor", None),
        P("replica", None, "tensor"),
    )
    return jax.shard_map(
        body,
        mesh=mesh,
        in_specs=placed,
        out_specs=(
            P("replica", None, "tensor"),
            P("replica", None, "tensor"),
            P("replica", None, "tensor"),
        ),
        check_vma=False,
    )
```

```python
import itertools
import math

import jax
import jax.numpy as jnp
from jax import lax
from jax.experimental import pallas as pl
from jax.experimental.pallas import tpu as pltpu
from jax.sharding import PartitionSpec as P

NZ, NX, NC, NY = 8, 4, 2, 8
PLANE = NX * NC
REPLICAS = NZ * PLANE
MESH = pl.DeviceIdType.MESH
F32, BF16 = jnp.float32, jnp.bfloat16

SLOTS, STEPS, BLOCKS, CACHE, HD, RANK = 16, 4, 4, 64, 128, 64
ROWS = SLOTS * STEPS
PART = 1024
HALF = ROWS // 2
MIG_ROWS = 2 * CACHE + 16
COPIES = 80

WIDE = PART + HD
MIG_TILES = MIG_ROWS // 16

ADAPTER_AT = {1: 0, 7: 1, 2: 2, 6: 3, 0: 4, 3: 5, 5: 6, 4: 7}
OWN, NEAR = 4, 5
X_AT = {0: 0, 1: 1, 2: 3, 3: 2}


def pick(table, index):
    out = jnp.int32(table[0])
    for key, value in table.items():
        if key:
            out = jnp.where(index == key, jnp.int32(value), out)
    return out


def lanes(shape):
    return lax.broadcasted_iota(jnp.int32, shape, len(shape) - 1)


def comm_kernel(
    tok_hbm, w_hbm, keys_hbm, values_hbm, length_hbm, mig_hbm, index_hbm, owner_hbm, shrink_hbm, expand_hbm,
    fresh_ref, arrived_ref,
    tok_ref, w_ref, keys_ref, values_ref, length_ref, mig_ref, index_ref, owner_ref, load_sem, tok_f32,
    tok_y, tok_x, adapter_z, expand_x, mig_out, mig_in, mig_z,
    acc, part_out, part_x, part_y, send_sem, recv_sem,
):
    r, t = lax.axis_index("replica"), lax.axis_index("tensor")
    z, w = r // PLANE, r % PLANE
    x, c = w // NC, w % NC

    def along_z(d):
        return ((r + d * PLANE) % REPLICAS, t)

    def along_y(d):
        return (r, (t + d) % NY)

    def in_plane(dx, dc):
        return (z * PLANE + ((x + dx) % NX) * NC + (c + dc) % NC, t)

    sibling = in_plane(0, 1)
    copies, numbers = [], itertools.count()

    def send(src, dst, device):
        k = next(numbers)
        copy = pltpu.make_async_remote_copy(
            src_ref=src, dst_ref=dst, send_sem=send_sem.at[k], recv_sem=recv_sem.at[k],
            device_id=device, device_id_type=MESH,
        )
        copies.append(copy)
        copy.start()
        return copy

    def plane_at(dx, dc):
        return dc * NX + X_AT[dx % NX]

    far_first = [(dx, dc) for dx in (2, 1, 3, 0) for dc in range(NC) if dx or dc]

    loads = [
        pltpu.make_async_copy(src, dst, load_sem.at[k])
        for k, (src, dst) in enumerate([
            (shrink_hbm, adapter_z.at[OWN, :, pl.ds(0, PART)]),
            (expand_hbm.at[0], adapter_z.at[OWN, :, pl.ds(PART, HD)]),
            (tok_hbm, tok_ref),
            (index_hbm, index_ref),
            (owner_hbm, owner_ref),
            (mig_hbm, mig_ref),
            (length_hbm, length_ref),
            (keys_hbm, keys_ref),
            (values_hbm, values_ref),
            (w_hbm, w_ref),
        ])
    ]
    load_w = loads.pop()
    for load in loads:
        load.start()

    barrier = pltpu.get_barrier_semaphore()
    others = [along_z(d) for d in (1, -1, 2, -2, NZ // 2)]
    others += [along_y(d) for d in range(1, NY)]
    others += [in_plane(dx, dc) for dx, dc in far_first]
    others += [((r + 1) % REPLICAS, t), ((r + REPLICAS - 1) % REPLICAS, t)]
    for other in others:
        pl.semaphore_signal(barrier, inc=1, device_id=other, device_id_type=MESH)

    def ring_of_8(to, views, halves):
        gone, last = {}, []
        for k in (1, 2, 3):
            for h, at in enumerate(views):
                for way in (-1, 1):
                    if k > 1:
                        gone[h, way].wait_recv()
                    gone[h, way] = send(at(way * (k - 1) % 8), at(way * k % 8), to(-way))
                if k == 3 and len(views) == 4:
                    way = (-1, -1, 1, 1)[h]
                    last.append(send(at(way * 2 % 8), at(4), to(-2 * way)))
            if k == 3 and len(views) == 1:
                last += [send(at(way * 2 % 8), at(4), to(-2 * way)) for way, at in zip((-1, 1), halves)]
            yield
        for copy in list(gone.values()):
            copy.wait_recv()
        yield
        for copy in last:
            copy.wait_recv()
        yield

    def ring_of_4(to, whole, halves):
        gone = {way: send(whole(0), whole(way % 4), to(-way)) for way in (-1, 1)}
        yield
        for copy in gone.values():
            copy.wait_recv()
        gone = [send(at(way % 4), at(2), to(-way)) for way, at in zip((-1, 1), halves)]
        yield
        for copy in gone:
            copy.wait_recv()
        yield

    def quarter(k):
        return lambda d: adapter_z.at[ADAPTER_AT[d], pl.ds(16 * k, 16)]

    z_steps = ring_of_8(along_z, [quarter(k) for k in range(4)], None)
    y_steps = ring_of_8(
        along_y,
        [lambda d: tok_y.at[d]],
        [lambda d: tok_y.at[d, pl.ds(0, HALF)], lambda d: tok_y.at[d, pl.ds(HALF, HALF)]],
    )
    x_steps = ring_of_4(
        lambda d: in_plane(d, 0),
        lambda d: tok_x.at[X_AT[d]],
        [lambda d: tok_x.at[X_AT[d], pl.ds(0, HALF)], lambda d: tok_x.at[X_AT[d], pl.ds(HALF, HALF + 16)]],
    )
    mig_steps = ring_of_8(
        along_z,
        [lambda d: mig_z.at[d]],
        [lambda d: mig_z.at[d, pl.ds(0, CACHE)], lambda d: mig_z.at[d, pl.ds(CACHE, MIG_ROWS - CACHE)]],
    )

    def to_plane(src, dst):
        return [send(src(plane_at(dx, dc)), dst(plane_at(-dx, dc)), in_plane(dx, dc)) for dx, dc in far_first]

    def expands_along_x(some):
        return [
            send(expand_x.at[0, some], expand_x.at[plane_at(-dx, 0), some], in_plane(dx, 0)) for dx in (2, 1, 3)
        ]

    def expands_over(some):
        return send(expand_x.at[pl.ds(0, NX), some], expand_x.at[pl.ds(NX, NX), some], sibling)

    base = None

    def add_base(d):
        nonlocal base
        rows = pl.multiple_of((t + d) % NY * PART, PART)
        term = jnp.dot(tok_y[d], w_ref[pl.ds(rows, PART), :], preferred_element_type=F32)
        base = term if base is None else base + term

    for load in loads[:2]:
        load.wait()
    pl.semaphore_wait(barrier, len(others))
    next(z_steps)

    for load in loads[2:]:
        load.wait()
    for s in range(SLOTS):
        tok_f32[s * STEPS : (s + 1) * STEPS, :] = tok_ref[s].astype(F32)
    own = tok_f32[...].astype(BF16)
    tok_x[0, 0:ROWS, 0:PART] = own
    row = lax.broadcasted_iota(jnp.int32, (ROWS, HD), 0)
    stored = [owner_ref[index_ref[0, b]] for b in range(BLOCKS)]
    stored_rows = jnp.zeros((ROWS, HD), F32)
    for b in range(BLOCKS):
        stored_rows = jnp.where(row // (ROWS // BLOCKS) == b, stored[b].astype(F32), stored_rows)
    tok_x[0, 0:ROWS, PART:] = stored_rows.astype(BF16)

    offsets = [(mig_ref[e, 0, 1] - r + REPLICAS) % REPLICAS for e in range(3)]
    half = REPLICAS // 2
    fits = [
        [o == 1 for o in offsets],
        [o == half for o in offsets],
        [(o != 1) & (o != half) for o in offsets],
    ]

    def chosen(which, column):
        first, second, third = (column(e) for e in range(3))
        return jnp.where(fits[which][0], first, jnp.where(fits[which][1], second, third))

    def leaving(which):
        slot = chosen(which, lambda e: mig_ref[e, 0, 0])
        landing = chosen(which, lambda e: mig_ref[e, 0, 2]).astype(F32)
        filled = length_ref[slot].astype(F32)
        notes = jnp.where(lax.broadcasted_iota(jnp.int32, (16, HD), 0) == 0, landing, filled)
        return jnp.concatenate([keys_ref[slot], values_ref[slot], notes.astype(BF16)], axis=0)

    other = leaving(2)
    for k in range(MIG_TILES):
        tok_x[0, ROWS:, k * HD : (k + 1) * HD] = other[k * 16 : (k + 1) * 16]
    next(x_steps)
    tok_y[0] = own
    next(y_steps)
    load_w.start()
    for which in range(2):
        mig_out[which] = leaving(which)
    straight = [send(mig_out.at[0], mig_in.at[0], ((r + 1) % REPLICAS, t))]
    load_w.wait()
    add_base(0)
    next(z_steps)
    next(x_steps)
    tokens_over = [send(tok_x.at[pl.ds(0, 3)], tok_x.at[pl.ds(NX, 3)], sibling)]
    next(y_steps)
    add_base(1)
    add_base(NY - 1)
    next(z_steps)
    next(x_steps)
    tokens_over += [send(tok_x.at[3], tok_x.at[NX + 3], sibling)]
    near, far = pl.ds(0, NEAR), pl.ds(NEAR, NZ - NEAR)
    expand_x[0, 0:NEAR] = adapter_z[0:NEAR, :, PART:]
    near_sent = expands_along_x(near)
    next(y_steps)
    for copy in tokens_over:
        copy.wait_recv()
    other_offset = chosen(2, lambda e: offsets[e])
    plane_offset, z_offset = other_offset % PLANE, other_offset // PLANE
    from_w = (w - plane_offset + PLANE) % PLANE
    carry = jnp.where(from_w + plane_offset >= PLANE, 1, 0)

    def plane_slot(place):
        return (place % NC - c + NC) % NC * NX + pick(X_AT, (place // NC - x + NX) % NX)

    from_slot = plane_slot(from_w)
    for k in range(MIG_TILES):
        mig_z[0, k * 16 : (k + 1) * 16] = tok_x[from_slot, ROWS:, k * HD : (k + 1) * HD]
    next(mig_steps)
    lane = lanes((1, HD))

    def add_products(pair, pairs):
        some = adapter_z[2 * pair : 2 * (pair + pairs), :, 0:PART].reshape(2 * pairs * RANK, PART)
        product = lax.dot_general(
            tok_x[:, 0:ROWS, 0:PART].reshape(PLANE * ROWS, PART), some, (((1,), (1,)), ((), ())),
            preferred_element_type=F32,
        )
        stored_all = tok_x[:, 0:ROWS, PART:].reshape(PLANE * ROWS, HD).astype(F32)
        out = None if pair == 0 else acc[...]
        for k in range(pairs):
            first, second = (
                ((r + d * PLANE) % REPLICAS).astype(F32) for d, at in ADAPTER_AT.items() if at // 2 == pair + k
            )
            mine = stored_all == jnp.where(lane < RANK, first, second)
            term = jnp.where(mine, product[:, k * HD : (k + 1) * HD], 0.0)
            out = term if out is None else out + term
        return out

    acc[...] = add_products(0, 2)

    next(z_steps)
    for copy in near_sent:
        copy.wait_recv()
    expand_over = [expands_over(near)]
    next(y_steps)
    next(mig_steps)
    add_base(2)
    add_base(NY - 2)
    acc[...] = add_products(2, 1)
    next(z_steps)

    total = add_products(3, 1).reshape(PLANE, ROWS, HD)
    total = total + jnp.concatenate([total[:, :, RANK:], total[:, :, :RANK]], axis=-1)
    total = jnp.where(lanes((PLANE, HALF, HD)) < RANK, total[:, :HALF], total[:, HALF:])
    part_out[...] = total.astype(BF16)
    part_sent = to_plane(lambda at: part_out.at[at], lambda at: part_x.at[at])
    expand_x[0, NEAR:] = adapter_z[NEAR:, :, PART:]
    far_sent = expands_along_x(far)
    part_x[0] = part_out[0]
    straight += [send(mig_out.at[1], mig_in.at[1], along_z(half // PLANE))]
    next(mig_steps)
    add_base(3)
    add_base(NY - 3)
    for copy in part_sent:
        copy.wait_recv()
    part_y[0] = jnp.sum(part_x[...].astype(F32), axis=0).astype(BF16)
    over_y = [send(part_y.at[0], part_y.at[NY - d], along_y(d)) for d in (4, 3, 5, 2, 6, 1, 7)]
    for copy in far_sent:
        copy.wait_recv()
    expand_over += [expands_over(far)]
    next(mig_steps)
    next(y_steps)
    add_base(4)
    next(mig_steps)
    from_z = (2 * NZ - z_offset - carry) % NZ
    arrived_ref[2] = mig_z[from_z]
    for k, copy in enumerate(straight):
        copy.wait_recv()
        arrived_ref[k] = mig_in[k]
    for copy in expand_over:
        copy.wait_recv()
    expands = [
        expand_x[plane_slot(stored[b] % PLANE), pick(ADAPTER_AT, (stored[b] // PLANE - z + NZ) % NZ)]
        for b in range(BLOCKS)
    ]
    for copy in copies:
        if not any(copy is one for one in over_y):
            copy.wait_send()
    for copy in over_y:
        copy.wait_recv()
    shrink = jnp.sum(part_y[...].astype(F32), axis=0).astype(BF16)
    rows = ROWS // BLOCKS
    lane16 = lanes((rows, HD))
    deltas = [None] * BLOCKS
    for k in range(2):
        mine = shrink[k * rows : (k + 1) * rows].astype(F32)
        left = jnp.where(lane16 < RANK, mine, 0.0)
        right = jnp.where(lane16 < RANK, 0.0, mine)
        both = jnp.concatenate([expands[k], expands[k + 2]], axis=0)
        out = jnp.dot(jnp.concatenate([left, right], axis=0).astype(BF16), both, preferred_element_type=F32)
        deltas[k], deltas[k + 2] = out[:rows], out[rows:]
    fresh_ref[...] = (base + jnp.concatenate(deltas, axis=0)).astype(BF16)

    for copy in over_y:
        copy.wait_send()


def attend_kernel(
    q_ref, draft_ref, keys_ref, values_ref, length_ref, arrived_ref, fresh_ref,
    out_hbm, ko_hbm, vo_hbm, out_ref, ko_ref, vo_ref, sem,
):
    group = q_ref.shape[2] // HD
    heads = group * STEPS
    spot = lax.broadcasted_iota(jnp.int32, (CACHE, HD), 0).astype(F32)
    landing = [arrived_ref[a, 2 * CACHE : 2 * CACHE + 1, :].astype(F32) for a in range(3)]
    lengths = [arrived_ref[a, 2 * CACHE + 1 : 2 * CACHE + 2, :].astype(F32) for a in range(3)]
    lane = lanes((1, HD))
    row_at = lax.broadcasted_iota(jnp.int32, (2 * heads, HD), 0)
    lane_at = lanes((2 * heads, HD))
    same = (row_at // heads) == (lane_at // CACHE)
    ahead = (lane_at % CACHE - row_at % STEPS).astype(F32)
    scale = 1.0 / math.sqrt(HD)
    pairs = range(SLOTS // 2)

    filled = []
    for s in range(SLOTS):
        fill = jnp.full((1, HD), length_ref[s].astype(F32))
        for a in range(3):
            fill = jnp.where(landing[a] == float(s), lengths[a], fill)
        filled.append(fill)

    def place(old_ref, first_row, new, out):
        for s in range(SLOTS):
            held = old_ref[s].astype(F32)
            for a in range(3):
                came = arrived_ref[a, first_row : first_row + CACHE].astype(F32)
                held = jnp.where(landing[a] == float(s), came, held)
            after = spot - filled[s]
            rows = new(s)
            for j in range(STEPS):
                held = jnp.where(after == float(j), rows[j : j + 1], held)
            out[s] = held.astype(BF16)

    place(keys_ref, 0, lambda s: draft_ref[s].astype(F32), ko_ref)
    keys_gone = pltpu.make_async_copy(ko_ref, ko_hbm, sem.at[0])
    keys_gone.start()
    scores = []
    for pair in pairs:
        queries = []
        for s in (2 * pair, 2 * pair + 1):
            query = q_ref[s].astype(F32)
            queries += [query[:, g * HD : (g + 1) * HD] for g in range(group)]
        stacked = jnp.concatenate(queries, axis=0).astype(BF16)
        both = ko_ref[2 * pair : 2 * pair + 2].reshape(2 * CACHE, HD)
        scores.append(lax.dot_general(stacked, both, (((1,), (1,)), ((), ())), preferred_element_type=F32) * scale)
    place(values_ref, CACHE, lambda s: fresh_ref[s * STEPS : (s + 1) * STEPS].astype(F32), vo_ref)
    values_gone = pltpu.make_async_copy(vo_ref, vo_hbm, sem.at[1])
    values_gone.start()
    weights = []
    for pair in pairs:
        allowed = same & (ahead <= jnp.where(lane < CACHE, filled[2 * pair], filled[2 * pair + 1]))
        masked = jnp.where(allowed, scores[pair], -1e30)
        top = jnp.max(masked, axis=-1, keepdims=True)
        raised = jnp.where(allowed, jnp.exp(masked - top), 0.0)
        weights.append((raised / jnp.sum(raised, axis=-1, keepdims=True)).astype(BF16))
    for pair in pairs:
        both = vo_ref[2 * pair : 2 * pair + 2].reshape(2 * CACHE, HD)
        attended = jnp.dot(weights[pair], both, preferred_element_type=F32)
        for k in range(2):
            for g in range(group):
                at = k * heads + g * STEPS
                out_ref[2 * pair + k, :, g * HD : (g + 1) * HD] = attended[at : at + STEPS].astype(BF16)
    out_gone = pltpu.make_async_copy(out_ref, out_hbm, sem.at[2])
    out_gone.start()
    keys_gone.wait()
    values_gone.wait()
    out_gone.wait()


def body(
    tokens,
    value_matrix,
    queries,
    draft_keys,
    key_cache_before,
    value_cache_before,
    cache_length,
    migrations,
    block_adapter_index,
    adapter_replica,
    adapter_shrink,
    adapter_expand,
):
    vmem = pl.BlockSpec(memory_space=pltpu.VMEM)
    hbm = pl.BlockSpec(memory_space=pltpu.HBM)
    smem = pl.BlockSpec(memory_space=pltpu.SMEM)
    fresh, arrived = pl.pallas_call(
        comm_kernel,
        out_shape=(
            jax.ShapeDtypeStruct((ROWS, HD), BF16),
            jax.ShapeDtypeStruct((3, MIG_ROWS, HD), BF16),
        ),
        in_specs=[hbm] * 10,
        out_specs=(vmem, vmem),
        scratch_shapes=[
            pltpu.VMEM(tokens.shape, BF16),
            pltpu.VMEM(value_matrix.shape, BF16),
            pltpu.VMEM(key_cache_before.shape, BF16),
            pltpu.VMEM(value_cache_before.shape, BF16),
            pltpu.SMEM(cache_length.shape, jnp.int32),
            pltpu.SMEM((3, 1, 3), jnp.int32),
            pltpu.SMEM(block_adapter_index.shape, jnp.int32),
            pltpu.SMEM(adapter_replica.shape, jnp.int32),
            pltpu.SemaphoreType.DMA((10,)),
            pltpu.VMEM((ROWS, PART), F32),
            pltpu.VMEM((NY, ROWS, PART), BF16),
            pltpu.VMEM((PLANE, ROWS + 16, WIDE), BF16),
            pltpu.VMEM((NZ, RANK, WIDE), BF16),
            pltpu.VMEM((PLANE, NZ, RANK, HD), BF16),
            pltpu.VMEM((2, MIG_ROWS, HD), BF16),
            pltpu.VMEM((2, MIG_ROWS, HD), BF16),
            pltpu.VMEM((NZ, MIG_ROWS, HD), BF16),
            pltpu.VMEM((PLANE * ROWS, HD), F32),
            pltpu.VMEM((PLANE, HALF, HD), BF16),
            pltpu.VMEM((PLANE, HALF, HD), BF16),
            pltpu.VMEM((NY, HALF, HD), BF16),
            pltpu.SemaphoreType.DMA((COPIES,)),
            pltpu.SemaphoreType.DMA((COPIES,)),
        ],
        compiler_params=pltpu.CompilerParams(
            collective_id=0, has_side_effects=True, vmem_limit_bytes=32 * 1024 * 1024
        ),
        name="gather_and_project",
    )(
        *(
            pltpu.with_memory_space_constraint(operand, pltpu.HBM)
            for operand in (
                tokens,
                value_matrix,
                key_cache_before,
                value_cache_before,
                cache_length,
                jnp.transpose(migrations, (1, 0, 2)),
                block_adapter_index,
                adapter_replica,
                jnp.swapaxes(adapter_shrink[0], 0, 1),
                adapter_expand,
            )
        )
    )
    return pl.pallas_call(
        attend_kernel,
        out_shape=(
            jax.ShapeDtypeStruct(queries.shape, BF16),
            jax.ShapeDtypeStruct(key_cache_before.shape, BF16),
            jax.ShapeDtypeStruct(value_cache_before.shape, BF16),
        ),
        in_specs=[vmem, vmem, vmem, vmem, smem, vmem, vmem],
        out_specs=(hbm, hbm, hbm),
        scratch_shapes=[
            pltpu.VMEM(queries.shape, BF16),
            pltpu.VMEM(key_cache_before.shape, BF16),
            pltpu.VMEM(value_cache_before.shape, BF16),
            pltpu.SemaphoreType.DMA((3,)),
        ],
        compiler_params=pltpu.CompilerParams(vmem_limit_bytes=24 * 1024 * 1024),
        name="place_and_attend",
    )(queries, draft_keys, key_cache_before, value_cache_before, cache_length, arrived, fresh)


def solution(mesh):
    placed = (
        P("replica", None, "tensor"),
        P(None, "tensor"),
        P("replica", None, "tensor"),
        P("replica", None, "tensor"),
        P("replica", None, "tensor"),
        P("replica", None, "tensor"),
        P("replica"),
        P("replica", None, None),
        P("replica", None),
        P(),
        P("replica", "tensor", None),
        P("replica", None, "tensor"),
    )
    return jax.shard_map(
        body,
        mesh=mesh,
        in_specs=placed,
        out_specs=(
            P("replica", None, "tensor"),
            P("replica", None, "tensor"),
            P("replica", None, "tensor"),
        ),
        check_vma=False,
    )
```

```python
import itertools
import math

import jax
import jax.numpy as jnp
from jax import lax
from jax.experimental import pallas as pl
from jax.experimental.pallas import tpu as pltpu
from jax.sharding import PartitionSpec as P

NZ, NX, NC, NY = 8, 4, 2, 8
PLANE = NX * NC
REPLICAS = NZ * PLANE
MESH = pl.DeviceIdType.MESH
F32, BF16 = jnp.float32, jnp.bfloat16

SLOTS, STEPS, BLOCKS, CACHE, HD, RANK = 16, 4, 4, 64, 128, 64
ROWS = SLOTS * STEPS
PART = 1024
HALF = ROWS // 2
MIG_ROWS = 2 * CACHE + 16
COPIES = 80

WIDE = PART + HD
MIG_TILES = MIG_ROWS // 16

ADAPTER_AT = {1: 0, 7: 1, 2: 2, 6: 3, 0: 4, 3: 5, 5: 6, 4: 7}
OWN, NEAR = 4, 5
X_AT = {0: 0, 1: 1, 2: 3, 3: 2}


def pick(table, index):
    out = jnp.int32(table[0])
    for key, value in table.items():
        if key:
            out = jnp.where(index == key, jnp.int32(value), out)
    return out


def lanes(shape):
    return lax.broadcasted_iota(jnp.int32, shape, len(shape) - 1)


class Placed:
    def __init__(self, arrived_ref, length_ref):
        self.arrived_ref = arrived_ref
        notes = [arrived_ref[a, 2 * CACHE :].astype(F32) for a in range(3)]
        self.landing = [rows[0:1] for rows in notes]
        self.filled = []
        for s in range(SLOTS):
            fill = jnp.full((1, HD), length_ref[s].astype(F32))
            for a in range(3):
                fill = jnp.where(self.landing[a] == float(s), notes[a][1:2], fill)
            self.filled.append(fill)

    def fill(self, old_ref, first_row, new, out_ref):
        spot = lax.broadcasted_iota(jnp.int32, (CACHE, HD), 0).astype(F32)
        for s in range(SLOTS):
            held = old_ref[s].astype(F32)
            for a in range(3):
                came = self.arrived_ref[a, first_row : first_row + CACHE].astype(F32)
                held = jnp.where(self.landing[a] == float(s), came, held)
            after = spot - self.filled[s]
            rows = new(s)
            for j in range(STEPS):
                held = jnp.where(after == float(j), rows[j : j + 1], held)
            out_ref[s] = held.astype(BF16)


def scores_and_weights(placed, q_ref, keys_ref, weights_ref):
    group = q_ref.shape[2] // HD
    heads = group * STEPS
    lane = lanes((1, HD))
    row_at = lax.broadcasted_iota(jnp.int32, (2 * heads, HD), 0)
    lane_at = lanes((2 * heads, HD))
    same = (row_at // heads) == (lane_at // CACHE)
    ahead = (lane_at % CACHE - row_at % STEPS).astype(F32)
    scale = 1.0 / math.sqrt(HD)
    scores = []
    for pair in range(SLOTS // 2):
        queries = []
        for s in (2 * pair, 2 * pair + 1):
            query = q_ref[s].astype(F32)
            queries += [query[:, g * HD : (g + 1) * HD] for g in range(group)]
        stacked = jnp.concatenate(queries, axis=0).astype(BF16)
        both = keys_ref[2 * pair : 2 * pair + 2].reshape(2 * CACHE, HD)
        scores.append(lax.dot_general(stacked, both, (((1,), (1,)), ((), ())), preferred_element_type=F32) * scale)
    for pair, score in enumerate(scores):
        allowed = same & (ahead <= jnp.where(lane < CACHE, placed.filled[2 * pair], placed.filled[2 * pair + 1]))
        masked = jnp.where(allowed, score, -1e30)
        top = jnp.max(masked, axis=-1, keepdims=True)
        raised = jnp.where(allowed, jnp.exp(masked - top), 0.0)
        weights_ref[pair] = (raised / jnp.sum(raised, axis=-1, keepdims=True)).astype(BF16)


def comm_kernel(
    tok_hbm, w_hbm, keys_hbm, values_hbm, length_hbm, mig_hbm, index_hbm, owner_hbm, shrink_hbm, expand_hbm,
    q_hbm, draft_hbm,
    fresh_ref, arrived_ref, ko_ref, weights_ref,
    q_ref, draft_ref, tok_ref, w_ref, keys_ref, values_ref, length_ref, mig_ref, index_ref, owner_ref, load_sem, tok_f32,
    tok_y, tok_x, adapter_z, expand_x, mig_out, mig_in, mig_z,
    acc, part_out, part_x, part_y, send_sem, recv_sem,
):
    r, t = lax.axis_index("replica"), lax.axis_index("tensor")
    z, w = r // PLANE, r % PLANE
    x, c = w // NC, w % NC

    def along_z(d):
        return ((r + d * PLANE) % REPLICAS, t)

    def along_y(d):
        return (r, (t + d) % NY)

    def in_plane(dx, dc):
        return (z * PLANE + ((x + dx) % NX) * NC + (c + dc) % NC, t)

    sibling = in_plane(0, 1)
    copies, numbers = [], itertools.count()

    def send(src, dst, device):
        k = next(numbers)
        copy = pltpu.make_async_remote_copy(
            src_ref=src, dst_ref=dst, send_sem=send_sem.at[k], recv_sem=recv_sem.at[k],
            device_id=device, device_id_type=MESH,
        )
        copies.append(copy)
        copy.start()
        return copy

    def plane_at(dx, dc):
        return dc * NX + X_AT[dx % NX]

    loads = [
        pltpu.make_async_copy(src, dst, load_sem.at[k])
        for k, (src, dst) in enumerate([
            (shrink_hbm, adapter_z.at[OWN, :, pl.ds(0, PART)]),
            (expand_hbm.at[0], adapter_z.at[OWN, :, pl.ds(PART, HD)]),
            (tok_hbm, tok_ref),
            (index_hbm, index_ref),
            (owner_hbm, owner_ref),
            (mig_hbm, mig_ref),
            (length_hbm, length_ref),
            (keys_hbm, keys_ref),
            (values_hbm, values_ref),
            (w_hbm, w_ref),
            (q_hbm, q_ref),
            (draft_hbm, draft_ref),
        ])
    ]
    late_loads = [loads.pop() for _ in range(3)]
    for load in loads:
        load.start()

    barrier = pltpu.get_barrier_semaphore()
    others = [along_z(1), along_z(-1), along_y(1), along_y(-1), in_plane(1, 0), in_plane(-1, 0), sibling]
    for other in others:
        pl.semaphore_signal(barrier, inc=1, device_id=other, device_id_type=MESH)

    def ring_of_8(to, views, halves):
        gone, last = {}, []
        for k in (1, 2, 3):
            for h, at in enumerate(views):
                for way in (-1, 1):
                    if k > 1:
                        gone[h, way].wait_recv()
                    gone[h, way] = send(at(way * (k - 1) % 8), at(way * k % 8), to(-way))
                if k == 3 and len(views) == 4:
                    way = (-1, -1, 1, 1)[h]
                    last.append(send(at(way * 2 % 8), at(4), to(-2 * way)))
            if k == 3 and len(views) == 1:
                last += [send(at(way * 2 % 8), at(4), to(-2 * way)) for way, at in zip((-1, 1), halves)]
            yield
        for copy in list(gone.values()):
            copy.wait_recv()
        yield
        for copy in last:
            copy.wait_recv()
        yield

    def ring_of_4(to, whole, halves):
        gone = {way: send(whole(0), whole(way % 4), to(-way)) for way in (-1, 1)}
        yield
        for copy in gone.values():
            copy.wait_recv()
        gone = [send(at(way % 4), at(2), to(-way)) for way, at in zip((-1, 1), halves)]
        yield
        for copy in gone:
            copy.wait_recv()
        yield

    def quarter(k):
        return lambda d: adapter_z.at[ADAPTER_AT[d], pl.ds(16 * k, 16)]

    z_steps = ring_of_8(along_z, [quarter(k) for k in range(4)], None)
    y_steps = ring_of_8(
        along_y,
        [lambda d: tok_y.at[d]],
        [lambda d: tok_y.at[d, pl.ds(0, HALF)], lambda d: tok_y.at[d, pl.ds(HALF, HALF)]],
    )
    x_steps = ring_of_4(
        lambda d: in_plane(d, 0),
        lambda d: tok_x.at[X_AT[d]],
        [lambda d: tok_x.at[X_AT[d], pl.ds(0, HALF)], lambda d: tok_x.at[X_AT[d], pl.ds(HALF, HALF + 16)]],
    )
    mig_steps = ring_of_8(
        along_z,
        [lambda d: mig_z.at[d]],
        [lambda d: mig_z.at[d, pl.ds(0, CACHE)], lambda d: mig_z.at[d, pl.ds(CACHE, MIG_ROWS - CACHE)]],
    )

    def expands_along_x(some):
        return [
            send(expand_x.at[0, some], expand_x.at[plane_at(-dx, 0), some], in_plane(dx, 0)) for dx in (2, 1, 3)
        ]

    def expands_over(some):
        return send(expand_x.at[pl.ds(0, NX), some], expand_x.at[pl.ds(NX, NX), some], sibling)

    base = None

    def add_base(d):
        nonlocal base
        rows = pl.multiple_of((t + d) % NY * PART, PART)
        term = jnp.dot(tok_y[d], w_ref[pl.ds(rows, PART), :], preferred_element_type=F32)
        base = term if base is None else base + term

    for load in loads[:2]:
        load.wait()
    pl.semaphore_wait(barrier, len(others))
    next(z_steps)

    for load in loads[2:]:
        load.wait()
    for s in range(SLOTS):
        tok_f32[s * STEPS : (s + 1) * STEPS, :] = tok_ref[s].astype(F32)
    own = tok_f32[...].astype(BF16)
    tok_x[0, 0:ROWS, 0:PART] = own
    row = lax.broadcasted_iota(jnp.int32, (ROWS, HD), 0)
    stored = [owner_ref[index_ref[0, b]] for b in range(BLOCKS)]
    stored_rows = jnp.zeros((ROWS, HD), F32)
    for b in range(BLOCKS):
        stored_rows = jnp.where(row // (ROWS // BLOCKS) == b, stored[b].astype(F32), stored_rows)
    tok_x[0, 0:ROWS, PART:] = stored_rows.astype(BF16)

    offsets = [(mig_ref[e, 0, 1] - r + REPLICAS) % REPLICAS for e in range(3)]
    half = REPLICAS // 2
    fits = [
        [o == 1 for o in offsets],
        [o == half for o in offsets],
        [(o != 1) & (o != half) for o in offsets],
    ]

    def chosen(which, column):
        first, second, third = (column(e) for e in range(3))
        return jnp.where(fits[which][0], first, jnp.where(fits[which][1], second, third))

    def leaving(which):
        slot = chosen(which, lambda e: mig_ref[e, 0, 0])
        landing = chosen(which, lambda e: mig_ref[e, 0, 2]).astype(F32)
        filled = length_ref[slot].astype(F32)
        notes = jnp.where(lax.broadcasted_iota(jnp.int32, (16, HD), 0) == 0, landing, filled)
        return jnp.concatenate([keys_ref[slot], values_ref[slot], notes.astype(BF16)], axis=0)

    other = leaving(2)
    for k in range(MIG_TILES):
        tok_x[0, ROWS:, k * HD : (k + 1) * HD] = other[k * 16 : (k + 1) * 16]
    next(x_steps)
    tok_y[0] = own
    next(y_steps)
    for load in late_loads:
        load.start()
    for which in range(2):
        mig_out[which] = leaving(which)
    for load in late_loads:
        load.wait()
    add_base(0)
    next(z_steps)
    next(x_steps)
    tokens_over = [send(tok_x.at[pl.ds(0, 3)], tok_x.at[pl.ds(NX, 3)], sibling)]
    next(y_steps)
    add_base(1)
    add_base(NY - 1)
    next(z_steps)
    next(x_steps)
    tokens_over += [send(tok_x.at[3], tok_x.at[NX + 3], sibling)]
    near, far = pl.ds(0, NEAR), pl.ds(NEAR, NZ - NEAR)
    expand_x[0, 0:NEAR] = adapter_z[0:NEAR, :, PART:]
    near_sent = expands_along_x(near)
    next(y_steps)
    for copy in tokens_over:
        copy.wait_recv()
    other_offset = chosen(2, lambda e: offsets[e])
    plane_offset, z_offset = other_offset % PLANE, other_offset // PLANE
    from_w = (w - plane_offset + PLANE) % PLANE
    carry = jnp.where(from_w + plane_offset >= PLANE, 1, 0)

    def plane_slot(place):
        return (place % NC - c + NC) % NC * NX + pick(X_AT, (place // NC - x + NX) % NX)

    from_slot = plane_slot(from_w)
    for k in range(MIG_TILES):
        mig_z[0, k * 16 : (k + 1) * 16] = tok_x[from_slot, ROWS:, k * HD : (k + 1) * HD]
    next(mig_steps)
    lane = lanes((1, HD))

    def add_products(pair, pairs):
        some = adapter_z[2 * pair : 2 * (pair + pairs), :, 0:PART].reshape(2 * pairs * RANK, PART)
        product = lax.dot_general(
            tok_x[:, 0:ROWS, 0:PART].reshape(PLANE * ROWS, PART), some, (((1,), (1,)), ((), ())),
            preferred_element_type=F32,
        )
        stored_all = tok_x[:, 0:ROWS, PART:].reshape(PLANE * ROWS, HD).astype(F32)
        out = None if pair == 0 else acc[...]
        for k in range(pairs):
            first, second = (
                ((r + d * PLANE) % REPLICAS).astype(F32) for d, at in ADAPTER_AT.items() if at // 2 == pair + k
            )
            mine = stored_all == jnp.where(lane < RANK, first, second)
            term = jnp.where(mine, product[:, k * HD : (k + 1) * HD], 0.0)
            out = term if out is None else out + term
        return out

    acc[...] = add_products(0, 2)

    next(z_steps)
    for copy in near_sent:
        copy.wait_recv()
    expand_over = [expands_over(near)]
    next(y_steps)
    next(mig_steps)
    add_base(2)
    add_base(NY - 2)
    acc[...] = add_products(2, 1)
    next(z_steps)

    some = adapter_z[NZ - 2 : NZ, :, 0:PART].reshape(2 * RANK, PART)
    nearer, farther = (((r + d * PLANE) % REPLICAS).astype(F32) for d in (5, 4))
    wanted = jnp.where(lane < RANK, nearer, farther)
    part_sent = []
    for dx in (2, 1, 3, 0):
        slots = [plane_at(dx, dc) for dc in range(NC)]
        product = lax.dot_general(
            jnp.concatenate([tok_x[at, 0:ROWS, 0:PART] for at in slots], axis=0), some, (((1,), (1,)), ((), ())),
            preferred_element_type=F32,
        )
        for dc, at in enumerate(slots):
            mine = tok_x[at, 0:ROWS, PART:].astype(F32) == wanted
            total = acc[at * ROWS : (at + 1) * ROWS] + jnp.where(mine, product[dc * ROWS : (dc + 1) * ROWS], 0.0)
            total = total + jnp.concatenate([total[:, RANK:], total[:, :RANK]], axis=-1)
            total = jnp.where(lanes((HALF, HD)) < RANK, total[:HALF], total[HALF:]).astype(BF16)
            if dx or dc:
                part_out[at] = total
                part_sent.append(send(part_out.at[at], part_x.at[plane_at(-dx, dc)], in_plane(dx, dc)))
            else:
                part_x[0] = total
    expand_x[0, NEAR:] = adapter_z[NEAR:, :, PART:]
    far_sent = expands_along_x(far)
    straight = [None, send(mig_out.at[1], mig_in.at[1], along_z(half // PLANE))]
    next(mig_steps)
    straight[0] = send(mig_out.at[0], mig_in.at[0], ((r + 1) % REPLICAS, t))
    add_base(3)
    add_base(NY - 3)
    for copy in part_sent:
        copy.wait_recv()
    next(y_steps)
    part_y[0] = jnp.sum(part_x[...].astype(F32), axis=0).astype(BF16)
    over_y = [send(part_y.at[0], part_y.at[NY - d], along_y(d)) for d in (4, 3, 5, 2, 6, 1, 7)]
    for copy in far_sent:
        copy.wait_recv()
    expand_over += [expands_over(far)]
    next(mig_steps)
    add_base(4)
    next(mig_steps)
    from_z = (2 * NZ - z_offset - carry) % NZ
    arrived_ref[2] = mig_z[from_z]
    for k, copy in enumerate(straight):
        copy.wait_recv()
        arrived_ref[k] = mig_in[k]
    placed = Placed(arrived_ref, length_ref)
    placed.fill(keys_ref, 0, lambda s: draft_ref[s].astype(F32), ko_ref)
    scores_and_weights(placed, q_ref, ko_ref, weights_ref)
    for copy in expand_over:
        copy.wait_recv()
    expands = [
        expand_x[plane_slot(stored[b] % PLANE), pick(ADAPTER_AT, (stored[b] // PLANE - z + NZ) % NZ)]
        for b in range(BLOCKS)
    ]
    for copy in copies:
        if not any(copy is one for one in over_y):
            copy.wait_send()
    for copy in over_y:
        copy.wait_recv()
    shrink = jnp.sum(part_y[...].astype(F32), axis=0).astype(BF16)
    rows = ROWS // BLOCKS
    lane16 = lanes((rows, HD))
    deltas = [None] * BLOCKS
    for k in range(2):
        mine = shrink[k * rows : (k + 1) * rows].astype(F32)
        left = jnp.where(lane16 < RANK, mine, 0.0)
        right = jnp.where(lane16 < RANK, 0.0, mine)
        both = jnp.concatenate([expands[k], expands[k + 2]], axis=0)
        out = jnp.dot(jnp.concatenate([left, right], axis=0).astype(BF16), both, preferred_element_type=F32)
        deltas[k], deltas[k + 2] = out[:rows], out[rows:]
    fresh_ref[...] = (base + jnp.concatenate(deltas, axis=0)).astype(BF16)

    for copy in over_y:
        copy.wait_send()


def attend_kernel(
    keys_ref, weights_ref, values_ref, length_ref, arrived_ref, fresh_ref,
    out_hbm, ko_hbm, vo_hbm, out_ref, vo_ref, sem,
):
    keys_gone = pltpu.make_async_copy(keys_ref, ko_hbm, sem.at[0])
    keys_gone.start()
    group = out_ref.shape[2] // HD
    heads = group * STEPS
    placed = Placed(arrived_ref, length_ref)
    placed.fill(
        values_ref, CACHE, lambda s: fresh_ref[s * STEPS : (s + 1) * STEPS].astype(F32), vo_ref
    )
    values_gone = pltpu.make_async_copy(vo_ref, vo_hbm, sem.at[1])
    values_gone.start()
    for pair in range(SLOTS // 2):
        both = vo_ref[2 * pair : 2 * pair + 2].reshape(2 * CACHE, HD)
        attended = jnp.dot(weights_ref[pair], both, preferred_element_type=F32)
        for k in range(2):
            for g in range(group):
                at = k * heads + g * STEPS
                out_ref[2 * pair + k, :, g * HD : (g + 1) * HD] = attended[at : at + STEPS].astype(BF16)
    out_gone = pltpu.make_async_copy(out_ref, out_hbm, sem.at[2])
    out_gone.start()
    keys_gone.wait()
    values_gone.wait()
    out_gone.wait()


def body(
    tokens,
    value_matrix,
    queries,
    draft_keys,
    key_cache_before,
    value_cache_before,
    cache_length,
    migrations,
    block_adapter_index,
    adapter_replica,
    adapter_shrink,
    adapter_expand,
):
    vmem = pl.BlockSpec(memory_space=pltpu.VMEM)
    hbm = pl.BlockSpec(memory_space=pltpu.HBM)
    smem = pl.BlockSpec(memory_space=pltpu.SMEM)
    fresh, arrived, keys_out, weights = pl.pallas_call(
        comm_kernel,
        out_shape=(
            jax.ShapeDtypeStruct((ROWS, HD), BF16),
            jax.ShapeDtypeStruct((3, MIG_ROWS, HD), BF16),
            jax.ShapeDtypeStruct(key_cache_before.shape, BF16),
            jax.ShapeDtypeStruct((SLOTS // 2, 2 * queries.shape[2] // HD * STEPS, 2 * CACHE), BF16),
        ),
        in_specs=[hbm] * 12,
        out_specs=(vmem, vmem, vmem, vmem),
        scratch_shapes=[
            pltpu.VMEM(queries.shape, BF16),
            pltpu.VMEM(draft_keys.shape, BF16),
            pltpu.VMEM(tokens.shape, BF16),
            pltpu.VMEM(value_matrix.shape, BF16),
            pltpu.VMEM(key_cache_before.shape, BF16),
            pltpu.VMEM(value_cache_before.shape, BF16),
            pltpu.SMEM(cache_length.shape, jnp.int32),
            pltpu.SMEM((3, 1, 3), jnp.int32),
            pltpu.SMEM(block_adapter_index.shape, jnp.int32),
            pltpu.SMEM(adapter_replica.shape, jnp.int32),
            pltpu.SemaphoreType.DMA((12,)),
            pltpu.VMEM((ROWS, PART), F32),
            pltpu.VMEM((NY, ROWS, PART), BF16),
            pltpu.VMEM((PLANE, ROWS + 16, WIDE), BF16),
            pltpu.VMEM((NZ, RANK, WIDE), BF16),
            pltpu.VMEM((PLANE, NZ, RANK, HD), BF16),
            pltpu.VMEM((2, MIG_ROWS, HD), BF16),
            pltpu.VMEM((2, MIG_ROWS, HD), BF16),
            pltpu.VMEM((NZ, MIG_ROWS, HD), BF16),
            pltpu.VMEM((PLANE * ROWS, HD), F32),
            pltpu.VMEM((PLANE, HALF, HD), BF16),
            pltpu.VMEM((PLANE, HALF, HD), BF16),
            pltpu.VMEM((NY, HALF, HD), BF16),
            pltpu.SemaphoreType.DMA((COPIES,)),
            pltpu.SemaphoreType.DMA((COPIES,)),
        ],
        compiler_params=pltpu.CompilerParams(
            collective_id=0, has_side_effects=True, vmem_limit_bytes=32 * 1024 * 1024
        ),
        name="gather_and_project",
    )(
        *(
            pltpu.with_memory_space_constraint(operand, pltpu.HBM)
            for operand in (
                tokens,
                value_matrix,
                key_cache_before,
                value_cache_before,
                cache_length,
                jnp.transpose(migrations, (1, 0, 2)),
                block_adapter_index,
                adapter_replica,
                jnp.swapaxes(adapter_shrink[0], 0, 1),
                adapter_expand,
                queries,
                draft_keys,
            )
        )
    )
    return pl.pallas_call(
        attend_kernel,
        out_shape=(
            jax.ShapeDtypeStruct(queries.shape, BF16),
            jax.ShapeDtypeStruct(key_cache_before.shape, BF16),
            jax.ShapeDtypeStruct(value_cache_before.shape, BF16),
        ),
        in_specs=[vmem, vmem, vmem, smem, vmem, vmem],
        out_specs=(hbm, hbm, hbm),
        scratch_shapes=[
            pltpu.VMEM(queries.shape, BF16),
            pltpu.VMEM(value_cache_before.shape, BF16),
            pltpu.SemaphoreType.DMA((3,)),
        ],
        compiler_params=pltpu.CompilerParams(vmem_limit_bytes=24 * 1024 * 1024),
        name="place_and_attend",
    )(keys_out, weights, value_cache_before, cache_length, arrived, fresh)


def solution(mesh):
    placed = (
        P("replica", None, "tensor"),
        P(None, "tensor"),
        P("replica", None, "tensor"),
        P("replica", None, "tensor"),
        P("replica", None, "tensor"),
        P("replica", None, "tensor"),
        P("replica"),
        P("replica", None, None),
        P("replica", None),
        P(),
        P("replica", "tensor", None),
        P("replica", None, "tensor"),
    )
    return jax.shard_map(
        body,
        mesh=mesh,
        in_specs=placed,
        out_specs=(
            P("replica", None, "tensor"),
            P("replica", None, "tensor"),
            P("replica", None, "tensor"),
        ),
        check_vma=False,
    )
```

```python
import itertools
import math

import jax
import jax.numpy as jnp
from jax import lax
from jax.experimental import pallas as pl
from jax.experimental.pallas import tpu as pltpu
from jax.sharding import PartitionSpec as P

NZ, NX, NC, NY = 8, 4, 2, 8
PLANE = NX * NC
REPLICAS = NZ * PLANE
MESH = pl.DeviceIdType.MESH
F32, BF16 = jnp.float32, jnp.bfloat16

SLOTS, STEPS, BLOCKS, CACHE, HD, RANK = 16, 4, 4, 64, 128, 64
ROWS = SLOTS * STEPS
PART = 1024
HALF = ROWS // 2
MIG_ROWS = 2 * CACHE + 16
COPIES = 80

WIDE = PART + HD
MIG_TILES = MIG_ROWS // 16

ADAPTER_AT = {1: 0, 7: 1, 2: 2, 6: 3, 0: 4, 3: 5, 5: 6, 4: 7}
OWN, NEAR = 4, 5
X_AT = {0: 0, 1: 1, 2: 3, 3: 2}


def pick(table, index):
    out = jnp.int32(table[0])
    for key, value in table.items():
        if key:
            out = jnp.where(index == key, jnp.int32(value), out)
    return out


def lanes(shape):
    return lax.broadcasted_iota(jnp.int32, shape, len(shape) - 1)


class Placed:
    def __init__(self, arrived_ref, length_ref):
        self.arrived_ref = arrived_ref
        notes = [arrived_ref[a, 2 * CACHE :].astype(F32) for a in range(3)]
        self.landing = [rows[0:1] for rows in notes]
        self.filled = []
        for s in range(SLOTS):
            fill = jnp.full((1, HD), length_ref[s].astype(F32))
            for a in range(3):
                fill = jnp.where(self.landing[a] == float(s), notes[a][1:2], fill)
            self.filled.append(fill)

    def fill(self, old_ref, first_row, new, out_ref):
        spot = lax.broadcasted_iota(jnp.int32, (CACHE, HD), 0).astype(F32)
        for s in range(SLOTS):
            held = old_ref[s].astype(F32)
            for a in range(3):
                came = self.arrived_ref[a, first_row : first_row + CACHE].astype(F32)
                held = jnp.where(self.landing[a] == float(s), came, held)
            after = spot - self.filled[s]
            rows = new(s)
            for j in range(STEPS):
                held = jnp.where(after == float(j), rows[j : j + 1], held)
            out_ref[s] = held.astype(BF16)


def scores_and_weights(placed, q_ref, keys_ref, weights_ref):
    group = q_ref.shape[2] // HD
    heads = group * STEPS
    lane = lanes((1, HD))
    row_at = lax.broadcasted_iota(jnp.int32, (2 * heads, HD), 0)
    lane_at = lanes((2 * heads, HD))
    same = (row_at // heads) == (lane_at // CACHE)
    ahead = (lane_at % CACHE - row_at % STEPS).astype(F32)
    scale = 1.0 / math.sqrt(HD)
    scores = []
    for pair in range(SLOTS // 2):
        queries = []
        for s in (2 * pair, 2 * pair + 1):
            query = q_ref[s].astype(F32)
            queries += [query[:, g * HD : (g + 1) * HD] for g in range(group)]
        stacked = jnp.concatenate(queries, axis=0).astype(BF16)
        both = keys_ref[2 * pair : 2 * pair + 2].reshape(2 * CACHE, HD)
        scores.append(lax.dot_general(stacked, both, (((1,), (1,)), ((), ())), preferred_element_type=F32) * scale)
    for pair, score in enumerate(scores):
        allowed = same & (ahead <= jnp.where(lane < CACHE, placed.filled[2 * pair], placed.filled[2 * pair + 1]))
        masked = jnp.where(allowed, score, -1e30)
        top = jnp.max(masked, axis=-1, keepdims=True)
        raised = jnp.where(allowed, jnp.exp(masked - top), 0.0)
        weights_ref[pair] = (raised / jnp.sum(raised, axis=-1, keepdims=True)).astype(BF16)


def comm_kernel(
    tok_hbm, w_hbm, keys_hbm, values_hbm, length_hbm, mig_hbm, index_hbm, owner_hbm, shrink_hbm, expand_hbm,
    q_hbm, draft_hbm,
    fresh_ref, arrived_ref, ko_ref, weights_ref,
    q_ref, draft_ref, tok_ref, w_ref, keys_ref, values_ref, length_ref, mig_ref, index_ref, owner_ref, load_sem, tok_f32,
    tok_y, tok_x, adapter_z, expand_x, mig_out, mig_in, mig_z,
    acc, part_out, part_x, part_y, send_sem, recv_sem,
):
    r, t = lax.axis_index("replica"), lax.axis_index("tensor")
    z, w = r // PLANE, r % PLANE
    x, c = w // NC, w % NC

    def along_z(d):
        return ((r + d * PLANE) % REPLICAS, t)

    def along_y(d):
        return (r, (t + d) % NY)

    def in_plane(dx, dc):
        return (z * PLANE + ((x + dx) % NX) * NC + (c + dc) % NC, t)

    sibling = in_plane(0, 1)
    copies, numbers = [], itertools.count()

    def send(src, dst, device):
        k = next(numbers)
        copy = pltpu.make_async_remote_copy(
            src_ref=src, dst_ref=dst, send_sem=send_sem.at[k], recv_sem=recv_sem.at[k],
            device_id=device, device_id_type=MESH,
        )
        copies.append(copy)
        copy.start()
        return copy

    def plane_at(dx, dc):
        return dc * NX + X_AT[dx % NX]

    settled = 0

    def settle(count):
        nonlocal settled
        for copy in copies[settled:count]:
            copy.wait_send()
        settled = max(settled, count)

    loads = [
        pltpu.make_async_copy(src, dst, load_sem.at[k])
        for k, (src, dst) in enumerate([
            (shrink_hbm, adapter_z.at[OWN, :, pl.ds(0, PART)]),
            (expand_hbm.at[0], adapter_z.at[OWN, :, pl.ds(PART, HD)]),
            (tok_hbm, tok_ref),
            (index_hbm, index_ref),
            (owner_hbm, owner_ref),
            (mig_hbm, mig_ref),
            (length_hbm, length_ref),
            (keys_hbm, keys_ref),
            (values_hbm, values_ref),
            (w_hbm, w_ref),
            (q_hbm, q_ref),
            (draft_hbm, draft_ref),
        ])
    ]
    late_loads = [loads.pop() for _ in range(3)]
    for load in loads:
        load.start()

    barrier = pltpu.get_barrier_semaphore()
    others = [along_z(1), along_z(-1), along_y(1), along_y(-1), in_plane(1, 0), in_plane(-1, 0), sibling]
    for other in others:
        pl.semaphore_signal(barrier, inc=1, device_id=other, device_id_type=MESH)

    def ring_of_8(to, views, halves):
        gone, last = {}, []
        for k in (1, 2, 3):
            for h, at in enumerate(views):
                for way in (-1, 1):
                    if k > 1:
                        gone[h, way].wait_recv()
                    gone[h, way] = send(at(way * (k - 1) % 8), at(way * k % 8), to(-way))
                if k == 3 and len(views) == 4:
                    way = (-1, -1, 1, 1)[h]
                    last.append(send(at(way * 2 % 8), at(4), to(-2 * way)))
            if k == 3 and len(views) == 1:
                last += [send(at(way * 2 % 8), at(4), to(-2 * way)) for way, at in zip((-1, 1), halves)]
            yield
        for copy in list(gone.values()):
            copy.wait_recv()
        yield
        for copy in last:
            copy.wait_recv()
        yield

    def ring_of_4(to, whole, halves):
        gone = {way: send(whole(0), whole(way % 4), to(-way)) for way in (-1, 1)}
        yield
        for copy in gone.values():
            copy.wait_recv()
        gone = [send(at(way % 4), at(2), to(-way)) for way, at in zip((-1, 1), halves)]
        yield
        for copy in gone:
            copy.wait_recv()
        yield

    def quarter(k):
        return lambda d: adapter_z.at[ADAPTER_AT[d], pl.ds(16 * k, 16)]

    z_steps = ring_of_8(along_z, [quarter(k) for k in range(4)], None)
    y_steps = ring_of_8(
        along_y,
        [lambda d: tok_y.at[d]],
        [lambda d: tok_y.at[d, pl.ds(0, HALF)], lambda d: tok_y.at[d, pl.ds(HALF, HALF)]],
    )
    x_steps = ring_of_4(
        lambda d: in_plane(d, 0),
        lambda d: tok_x.at[X_AT[d]],
        [lambda d: tok_x.at[X_AT[d], pl.ds(0, HALF)], lambda d: tok_x.at[X_AT[d], pl.ds(HALF, HALF + 16)]],
    )
    mig_steps = ring_of_8(
        along_z,
        [lambda d: mig_z.at[d]],
        [lambda d: mig_z.at[d, pl.ds(0, CACHE)], lambda d: mig_z.at[d, pl.ds(CACHE, MIG_ROWS - CACHE)]],
    )

    def expands_along_x(some):
        return [
            send(expand_x.at[0, some], expand_x.at[plane_at(-dx, 0), some], in_plane(dx, 0)) for dx in (2, 1, 3)
        ]

    def expands_over(some):
        return send(expand_x.at[pl.ds(0, NX), some], expand_x.at[pl.ds(NX, NX), some], sibling)

    base = None

    def add_base(d):
        nonlocal base
        rows = pl.multiple_of((t + d) % NY * PART, PART)
        term = jnp.dot(tok_y[d], w_ref[pl.ds(rows, PART), :], preferred_element_type=F32)
        base = term if base is None else base + term

    for load in loads[:2]:
        load.wait()
    pl.semaphore_wait(barrier, len(others))
    next(z_steps)

    for load in loads[2:]:
        load.wait()
    for s in range(SLOTS):
        tok_f32[s * STEPS : (s + 1) * STEPS, :] = tok_ref[s].astype(F32)
    own = tok_f32[...].astype(BF16)
    tok_x[0, 0:ROWS, 0:PART] = own
    row = lax.broadcasted_iota(jnp.int32, (ROWS, HD), 0)
    stored = [owner_ref[index_ref[0, b]] for b in range(BLOCKS)]
    stored_rows = jnp.zeros((ROWS, HD), F32)
    for b in range(BLOCKS):
        stored_rows = jnp.where(row // (ROWS // BLOCKS) == b, stored[b].astype(F32), stored_rows)
    tok_x[0, 0:ROWS, PART:] = stored_rows.astype(BF16)

    offsets = [(mig_ref[e, 0, 1] - r + REPLICAS) % REPLICAS for e in range(3)]
    half = REPLICAS // 2
    fits = [
        [o == 1 for o in offsets],
        [o == half for o in offsets],
        [(o != 1) & (o != half) for o in offsets],
    ]

    def chosen(which, column):
        first, second, third = (column(e) for e in range(3))
        return jnp.where(fits[which][0], first, jnp.where(fits[which][1], second, third))

    def leaving(which):
        slot = chosen(which, lambda e: mig_ref[e, 0, 0])
        landing = chosen(which, lambda e: mig_ref[e, 0, 2]).astype(F32)
        filled = length_ref[slot].astype(F32)
        notes = jnp.where(lax.broadcasted_iota(jnp.int32, (16, HD), 0) == 0, landing, filled)
        return jnp.concatenate([keys_ref[slot], values_ref[slot], notes.astype(BF16)], axis=0)

    other = leaving(2)
    for k in range(MIG_TILES):
        tok_x[0, ROWS:, k * HD : (k + 1) * HD] = other[k * 16 : (k + 1) * 16]
    next(x_steps)
    tok_y[0] = own
    next(y_steps)
    for load in late_loads:
        load.start()
    for which in range(2):
        mig_out[which] = leaving(which)
    for load in late_loads:
        load.wait()
    add_base(0)
    next(z_steps)
    next(x_steps)
    tokens_over = [send(tok_x.at[pl.ds(0, 3)], tok_x.at[pl.ds(NX, 3)], sibling)]
    next(y_steps)
    add_base(1)
    add_base(NY - 1)
    before_3 = len(copies)
    next(z_steps)
    next(x_steps)
    tokens_over += [send(tok_x.at[3], tok_x.at[NX + 3], sibling)]
    near, far = pl.ds(0, NEAR), pl.ds(NEAR, NZ - NEAR)
    expand_x[0, 0:NEAR] = adapter_z[0:NEAR, :, PART:]
    near_sent = expands_along_x(near)
    next(y_steps)
    for copy in tokens_over:
        copy.wait_recv()
    other_offset = chosen(2, lambda e: offsets[e])
    plane_offset, z_offset = other_offset % PLANE, other_offset // PLANE
    from_w = (w - plane_offset + PLANE) % PLANE
    carry = jnp.where(from_w + plane_offset >= PLANE, 1, 0)

    def plane_slot(place):
        return (place % NC - c + NC) % NC * NX + pick(X_AT, (place // NC - x + NX) % NX)

    from_slot = plane_slot(from_w)
    for k in range(MIG_TILES):
        mig_z[0, k * 16 : (k + 1) * 16] = tok_x[from_slot, ROWS:, k * HD : (k + 1) * HD]
    next(mig_steps)
    lane = lanes((1, HD))

    def add_products(pair, pairs):
        some = adapter_z[2 * pair : 2 * (pair + pairs), :, 0:PART].reshape(2 * pairs * RANK, PART)
        product = lax.dot_general(
            tok_x[:, 0:ROWS, 0:PART].reshape(PLANE * ROWS, PART), some, (((1,), (1,)), ((), ())),
            preferred_element_type=F32,
        )
        stored_all = tok_x[:, 0:ROWS, PART:].reshape(PLANE * ROWS, HD).astype(F32)
        out = None if pair == 0 else acc[...]
        for k in range(pairs):
            first, second = (
                ((r + d * PLANE) % REPLICAS).astype(F32) for d, at in ADAPTER_AT.items() if at // 2 == pair + k
            )
            mine = stored_all == jnp.where(lane < RANK, first, second)
            term = jnp.where(mine, product[:, k * HD : (k + 1) * HD], 0.0)
            out = term if out is None else out + term
        return out

    acc[...] = add_products(0, 2)

    next(z_steps)
    for copy in near_sent:
        copy.wait_recv()
    expand_over = [expands_over(near)]
    next(y_steps)
    next(mig_steps)
    add_base(2)
    add_base(NY - 2)
    acc[...] = add_products(2, 1)
    before_last = len(copies)
    settle(before_3)
    next(z_steps)

    some = adapter_z[NZ - 2 : NZ, :, 0:PART].reshape(2 * RANK, PART)
    nearer, farther = (((r + d * PLANE) % REPLICAS).astype(F32) for d in (5, 4))
    wanted = jnp.where(lane < RANK, nearer, farther)
    part_sent = []
    for dx in (2, 1, 3, 0):
        slots = [plane_at(dx, dc) for dc in range(NC)]
        product = lax.dot_general(
            jnp.concatenate([tok_x[at, 0:ROWS, 0:PART] for at in slots], axis=0), some, (((1,), (1,)), ((), ())),
            preferred_element_type=F32,
        )
        for dc, at in enumerate(slots):
            mine = tok_x[at, 0:ROWS, PART:].astype(F32) == wanted
            total = acc[at * ROWS : (at + 1) * ROWS] + jnp.where(mine, product[dc * ROWS : (dc + 1) * ROWS], 0.0)
            total = total + jnp.concatenate([total[:, RANK:], total[:, :RANK]], axis=-1)
            total = jnp.where(lanes((HALF, HD)) < RANK, total[:HALF], total[HALF:]).astype(BF16)
            if dx or dc:
                part_out[at] = total
                part_sent.append(send(part_out.at[at], part_x.at[plane_at(-dx, dc)], in_plane(dx, dc)))
            else:
                part_x[0] = total
    expand_x[0, NEAR:] = adapter_z[NEAR:, :, PART:]
    far_sent = expands_along_x(far)
    straight = [None, send(mig_out.at[1], mig_in.at[1], along_z(half // PLANE))]
    next(mig_steps)
    straight[0] = send(mig_out.at[0], mig_in.at[0], ((r + 1) % REPLICAS, t))
    settle(before_last)
    for copy in part_sent:
        copy.wait_recv()
    next(y_steps)
    part_y[0] = jnp.sum(part_x[...].astype(F32), axis=0).astype(BF16)
    before_y = len(copies)
    over_y = [send(part_y.at[0], part_y.at[NY - d], along_y(d)) for d in (4, 3, 5, 2, 6, 1, 7)]
    for copy in far_sent:
        copy.wait_recv()
    expand_over += [expands_over(far)]
    next(mig_steps)
    add_base(3)
    add_base(NY - 3)
    add_base(4)
    next(mig_steps)
    from_z = (2 * NZ - z_offset - carry) % NZ
    arrived_ref[2] = mig_z[from_z]
    for k, copy in enumerate(straight):
        copy.wait_recv()
        arrived_ref[k] = mig_in[k]
    placed = Placed(arrived_ref, length_ref)
    placed.fill(keys_ref, 0, lambda s: draft_ref[s].astype(F32), ko_ref)
    scores_and_weights(placed, q_ref, ko_ref, weights_ref)
    for copy in expand_over:
        copy.wait_recv()
    expands = [
        expand_x[plane_slot(stored[b] % PLANE), pick(ADAPTER_AT, (stored[b] // PLANE - z + NZ) % NZ)]
        for b in range(BLOCKS)
    ]
    settle(before_y)
    for copy in over_y:
        copy.wait_recv()
    shrink = jnp.sum(part_y[...].astype(F32), axis=0).astype(BF16)
    rows = ROWS // BLOCKS
    lane16 = lanes((rows, HD))
    deltas = [None] * BLOCKS
    for k in range(2):
        mine = shrink[k * rows : (k + 1) * rows].astype(F32)
        left = jnp.where(lane16 < RANK, mine, 0.0)
        right = jnp.where(lane16 < RANK, 0.0, mine)
        both = jnp.concatenate([expands[k], expands[k + 2]], axis=0)
        out = jnp.dot(jnp.concatenate([left, right], axis=0).astype(BF16), both, preferred_element_type=F32)
        deltas[k], deltas[k + 2] = out[:rows], out[rows:]
    fresh_ref[...] = (base + jnp.concatenate(deltas, axis=0)).astype(BF16)

    settle(len(copies))


def attend_kernel(
    keys_ref, weights_ref, values_ref, length_ref, arrived_ref, fresh_ref,
    out_hbm, ko_hbm, vo_hbm, out_ref, vo_ref, sem,
):
    keys_gone = pltpu.make_async_copy(keys_ref, ko_hbm, sem.at[0])
    keys_gone.start()
    group = out_ref.shape[2] // HD
    heads = group * STEPS
    placed = Placed(arrived_ref, length_ref)
    placed.fill(
        values_ref, CACHE, lambda s: fresh_ref[s * STEPS : (s + 1) * STEPS].astype(F32), vo_ref
    )
    values_gone = pltpu.make_async_copy(vo_ref, vo_hbm, sem.at[1])
    values_gone.start()
    for pair in range(SLOTS // 2):
        both = vo_ref[2 * pair : 2 * pair + 2].reshape(2 * CACHE, HD)
        attended = jnp.dot(weights_ref[pair], both, preferred_element_type=F32)
        for k in range(2):
            for g in range(group):
                at = k * heads + g * STEPS
                out_ref[2 * pair + k, :, g * HD : (g + 1) * HD] = attended[at : at + STEPS].astype(BF16)
    out_gone = pltpu.make_async_copy(out_ref, out_hbm, sem.at[2])
    out_gone.start()
    keys_gone.wait()
    values_gone.wait()
    out_gone.wait()


def body(
    tokens,
    value_matrix,
    queries,
    draft_keys,
    key_cache_before,
    value_cache_before,
    cache_length,
    migrations,
    block_adapter_index,
    adapter_replica,
    adapter_shrink,
    adapter_expand,
):
    vmem = pl.BlockSpec(memory_space=pltpu.VMEM)
    hbm = pl.BlockSpec(memory_space=pltpu.HBM)
    smem = pl.BlockSpec(memory_space=pltpu.SMEM)
    fresh, arrived, keys_out, weights = pl.pallas_call(
        comm_kernel,
        out_shape=(
            jax.ShapeDtypeStruct((ROWS, HD), BF16),
            jax.ShapeDtypeStruct((3, MIG_ROWS, HD), BF16),
            jax.ShapeDtypeStruct(key_cache_before.shape, BF16),
            jax.ShapeDtypeStruct((SLOTS // 2, 2 * queries.shape[2] // HD * STEPS, 2 * CACHE), BF16),
        ),
        in_specs=[hbm] * 12,
        out_specs=(vmem, vmem, vmem, vmem),
        scratch_shapes=[
            pltpu.VMEM(queries.shape, BF16),
            pltpu.VMEM(draft_keys.shape, BF16),
            pltpu.VMEM(tokens.shape, BF16),
            pltpu.VMEM(value_matrix.shape, BF16),
            pltpu.VMEM(key_cache_before.shape, BF16),
            pltpu.VMEM(value_cache_before.shape, BF16),
            pltpu.SMEM(cache_length.shape, jnp.int32),
            pltpu.SMEM((3, 1, 3), jnp.int32),
            pltpu.SMEM(block_adapter_index.shape, jnp.int32),
            pltpu.SMEM(adapter_replica.shape, jnp.int32),
            pltpu.SemaphoreType.DMA((12,)),
            pltpu.VMEM((ROWS, PART), F32),
            pltpu.VMEM((NY, ROWS, PART), BF16),
            pltpu.VMEM((PLANE, ROWS + 16, WIDE), BF16),
            pltpu.VMEM((NZ, RANK, WIDE), BF16),
            pltpu.VMEM((PLANE, NZ, RANK, HD), BF16),
            pltpu.VMEM((2, MIG_ROWS, HD), BF16),
            pltpu.VMEM((2, MIG_ROWS, HD), BF16),
            pltpu.VMEM((NZ, MIG_ROWS, HD), BF16),
            pltpu.VMEM((PLANE * ROWS, HD), F32),
            pltpu.VMEM((PLANE, HALF, HD), BF16),
            pltpu.VMEM((PLANE, HALF, HD), BF16),
            pltpu.VMEM((NY, HALF, HD), BF16),
            pltpu.SemaphoreType.DMA((COPIES,)),
            pltpu.SemaphoreType.DMA((COPIES,)),
        ],
        compiler_params=pltpu.CompilerParams(
            collective_id=0, has_side_effects=True, vmem_limit_bytes=32 * 1024 * 1024
        ),
        name="gather_and_project",
    )(
        *(
            pltpu.with_memory_space_constraint(operand, pltpu.HBM)
            for operand in (
                tokens,
                value_matrix,
                key_cache_before,
                value_cache_before,
                cache_length,
                jnp.transpose(migrations, (1, 0, 2)),
                block_adapter_index,
                adapter_replica,
                jnp.swapaxes(adapter_shrink[0], 0, 1),
                adapter_expand,
                queries,
                draft_keys,
            )
        )
    )
    return pl.pallas_call(
        attend_kernel,
        out_shape=(
            jax.ShapeDtypeStruct(queries.shape, BF16),
            jax.ShapeDtypeStruct(key_cache_before.shape, BF16),
            jax.ShapeDtypeStruct(value_cache_before.shape, BF16),
        ),
        in_specs=[vmem, vmem, vmem, smem, vmem, vmem],
        out_specs=(hbm, hbm, hbm),
        scratch_shapes=[
            pltpu.VMEM(queries.shape, BF16),
            pltpu.VMEM(value_cache_before.shape, BF16),
            pltpu.SemaphoreType.DMA((3,)),
        ],
        compiler_params=pltpu.CompilerParams(vmem_limit_bytes=24 * 1024 * 1024),
        name="place_and_attend",
    )(keys_out, weights, value_cache_before, cache_length, arrived, fresh)


def solution(mesh):
    placed = (
        P("replica", None, "tensor"),
        P(None, "tensor"),
        P("replica", None, "tensor"),
        P("replica", None, "tensor"),
        P("replica", None, "tensor"),
        P("replica", None, "tensor"),
        P("replica"),
        P("replica", None, None),
        P("replica", None),
        P(),
        P("replica", "tensor", None),
        P("replica", None, "tensor"),
    )
    return jax.shard_map(
        body,
        mesh=mesh,
        in_specs=placed,
        out_specs=(
            P("replica", None, "tensor"),
            P("replica", None, "tensor"),
            P("replica", None, "tensor"),
        ),
        check_vma=False,
    )
```
